256 devices in a mesh: rows: 16 (over y, x), cols: 16 (over z, core).
Axes of the slice: x: 4, y: 4, z: 8, core: 2. Of those that a mesh axis runs over, the one named last changes fastest.
Arguments:
- right_side: float32 [8, 512, 8192], P(None, 'rows', 'cols'), may hold values from -30 to 30
- east_class: int32 [512, 8192], P('rows', 'cols'), may hold values from 0 to 15
- lower_class: int32 [512, 8192], P('rows', 'cols'), may hold values from 0 to 15
- via_mask: int32 [512, 8192], P('rows', 'cols'), may hold values 0 or 1
- class_conductance: float32 [16], replicated, may hold values from 0.5 to 2
Outputs:
- solution_field: float32 [8, 512, 8192], P(None, 'rows', 'cols')
- residual: float32 [8, 512, 8192], P(None, 'rows', 'cols')
The draws below stay inside these ranges and needn't reach their ends.
All inputs are finite; a program needn't handle non-finite values. No bound on the sum of `via_mask` on one device may be relied on, other than what follows from the above.
Results may differ from the reference program's by a relative error of at most 0.007.
Values sent between devices are 32-bit elements; how exact they have to be, the bound alone decides.
A program may use at most 64 MiB of HBM per device.

```python
import math
import jax
import jax.numpy as jnp
from jax import lax

K = 8
S = 5
OUTER = 2
NCLASS = 16
NR = 512
NC = 8192


def draw_right_side(key, part):
    key = jax.random.fold_in(key, 11)
    first, second = jax.random.split(key, 2)
    shape = (K, NR, NC)
    row_pos = jnp.arange(NR, dtype=jnp.float32)[:, None] / NR
    col_pos = jnp.arange(NC, dtype=jnp.float32)[None, :] / NC
    ramp = (1.0 + row_pos) * (1.0 + 2.0 * col_pos)
    rough = jnp.exp(jax.random.uniform(second, shape, jnp.float32, 0.0, math.log(10.0)))
    base = jax.random.normal(first, shape, jnp.float32)
    return jnp.clip(0.25 * base * rough * ramp, -30.0, 30.0)


def touch_ends(drawn, rng, low, high):
    longest = drawn.shape.index(max(drawn.shape))
    spots = []
    for shift in (0, 1):
        where = [jax.random.randint(jax.random.fold_in(rng, axis), (), 0, length) for axis, length in enumerate(drawn.shape)]
        where[longest] = (where[longest] + shift) % drawn.shape[longest]
        spots.append(tuple(where))
    return drawn.at[spots[0]].set(low).at[spots[1]].set(high)


def setup_inputs(seed: int = 0) -> dict:
    splits = jax.random.split(jax.random.key(seed), 6)
    right_side = draw_right_side(jax.random.fold_in(splits[5], 71), 0)
    east_class = touch_ends(jax.random.randint(splits[1], (NR, NC), 0, NCLASS), jax.random.fold_in(splits[1], 1), 0, NCLASS - 1).astype(jnp.int32)
    lower_class = touch_ends(jax.random.randint(splits[2], (NR, NC), 0, NCLASS), jax.random.fold_in(splits[2], 1), 0, NCLASS - 1).astype(jnp.int32)
    via_mask = touch_ends((jax.random.randint(splits[3], (NR, NC), 0, 6) < 1).astype(jnp.int32), jax.random.fold_in(splits[3], 1), 0, 1)
    class_conductance = jnp.clip(jnp.exp(jax.random.uniform(splits[4], (NCLASS,), jnp.float32, math.log(0.5), math.log(2.0))), 0.5, 2.0)
    return {"right_side": right_side, "east_class": east_class, "lower_class": lower_class, "via_mask": via_mask, "class_conductance": class_conductance}


LEAK = 0.05
PAD_G = 2.0
SHIFT = 6.0
SCALE = 1.0 / 6.0

def lookup(classes, table):
    hits = (classes[..., None] == jnp.arange(table.shape[0], dtype=jnp.int32)).astype(jnp.float32)
    return lax.optimization_barrier(jnp.sum(hits * table, axis=-1))

def stencil(field, east_edge, lower_edge, padterm):
    padded = jnp.pad(field, ((0, 0), (1, 1), (1, 1)))
    west_edge = jnp.pad(east_edge, ((0, 0), (1, 0)))[:, :-1]
    upper_edge = jnp.pad(lower_edge, ((1, 0), (0, 0)))[:-1, :]
    center = east_edge + west_edge + lower_edge + upper_edge + padterm + LEAK
    return center * field - east_edge * padded[:, 1:-1, 2:] - west_edge * padded[:, 1:-1, :-2] - lower_edge * padded[:, 2:, 1:-1] - upper_edge * padded[:, :-2, 1:-1]

def inner_block(left, right):
    return lax.dot_general(left.reshape(left.shape[0], -1).astype(jnp.float32), right.reshape(right.shape[0], -1).astype(jnp.float32), (((1,), (1,)), ((), ())), precision=lax.Precision.HIGHEST, preferred_element_type=jnp.float32)

def solve_small(gram, projected):
    sym = 0.5 * (gram + gram.T)
    weight = lax.rsqrt(jnp.diagonal(sym))
    scaled = sym * weight[:, None] * weight[None, :]
    factor = jnp.linalg.cholesky(scaled)
    return weight[:, None] * jax.scipy.linalg.cho_solve((factor, True), weight[:, None] * projected)

def reference(right_side, east_class, lower_class, via_mask, class_conductance):
    loads, total_rows, total_cols = right_side.shape
    col_keep = (jnp.arange(total_cols, dtype=jnp.int32) < total_cols - 1).astype(jnp.float32)
    row_keep = (jnp.arange(total_rows, dtype=jnp.int32) < total_rows - 1).astype(jnp.float32)
    east_edge = lookup(east_class, class_conductance) * col_keep[None, :]
    lower_edge = lookup(lower_class, class_conductance) * row_keep[:, None]
    padterm = PAD_G * via_mask.astype(jnp.float32)
    solution_field = jnp.zeros_like(right_side)
    residual = right_side
    for sweep in range(OUTER):
        basis = []
        images = []
        current = residual
        for level in range(S):
            image = stencil(current, east_edge, lower_edge, padterm)
            basis.append(current)
            images.append(image)
            current = (image - SHIFT * current) * SCALE
        gram = jnp.concatenate([jnp.concatenate([inner_block(basis[first], images[second]) for second in range(S)], axis=1) for first in range(S)], axis=0)
        projected = jnp.concatenate([inner_block(basis[first], residual) for first in range(S)], axis=0)
        coefficients = solve_small(gram, projected)
        for level in range(S):
            part = coefficients[level * loads:(level + 1) * loads]
            solution_field = solution_field + jnp.einsum('mk,mxy->kxy', part, basis[level], precision=lax.Precision.HIGHEST)
            residual = residual - jnp.einsum('mk,mxy->kxy', part, images[level], precision=lax.Precision.HIGHEST)
    return (solution_field, residual)
```

```python
import functools

import jax
import jax.numpy as jnp
from jax import lax
from jax.experimental import pallas as pl
from jax.experimental.pallas import tpu as pltpu
from jax.sharding import PartitionSpec as P

S = 5
OUTER = 2
D = S * OUTER
LEAK = 0.05
PAD_G = 2.0
SHIFT = 6.0
LANES = 128
CH = 16
MOMENTS = 14
SHIFTS = 5
f32 = jnp.float32
MESH = pl.DeviceIdType.MESH


def lane_bc(x, lane):
    return jnp.broadcast_to(x[:, lane : lane + 1], x.shape)


def row_bc(x, row):
    return jnp.broadcast_to(x[row : row + 1, :], x.shape)


def stencil_rows(src, dst, E, L, C, first, count):
    width = src.shape[-1]
    below = L[first - 1] * src[first - 1]
    for q in range(count):
        i = first + q
        v = src[i]
        e = E[i]
        l = L[i]
        dst[i] = (C[i] * v - e * pltpu.roll(v, width - 1, 1)) - (
            pltpu.roll(e * v, 1, 1) + (l * src[i + 1] + below)
        )
        below = l * v


def moments(V, first, rows, own):
    tiles = {}
    for s0, s1 in ((0, 3), (3, SHIFTS)):

        def row(i, acc):
            acc = list(acc)
            for t in range(own // LANES):
                sl = pl.ds(LANES * t, LANES)
                b = [V[m, i, :, sl] for m in range(S + 1)]
                w = [b[m] + b[m + 1] for m in range(S)]
                for s in range(s0, s1):
                    r = [b[m] if s == 0 else pltpu.roll(b[m], s, 0) for m in range(S)]
                    j = (s - s0) * MOMENTS
                    for k in range(2 * S - 1):
                        acc[j + k] = acc[j + k] + r[k // 2] * w[k - k // 2]
                    for k in range(S):
                        acc[j + 9 + k] = acc[j + 9 + k] + r[k // 2] * b[k - k // 2]
            return tuple(acc)

        zero = jnp.zeros((8, LANES), f32)
        acc = lax.fori_loop(first, first + rows, row, (zero,) * (MOMENTS * (s1 - s0)))
        for s in range(s0, s1):
            for k in range(MOMENTS):
                tiles[s, k] = acc[(s - s0) * MOMENTS + k]
    lane = lax.broadcasted_iota(jnp.int32, (8, LANES), 1)
    out = jnp.zeros((8, LANES), f32)
    for (s, k), x in tiles.items():
        total = jnp.broadcast_to(jnp.sum(x, axis=1, keepdims=True), x.shape)
        out = jnp.where(lane == s * MOMENTS + k, total, out)
    return out


def solve(packed):
    lane = lax.broadcasted_iota(jnp.int32, (8, LANES), 1)
    sub = lax.broadcasted_iota(jnp.int32, (8, LANES), 0)
    gap = (sub - lane) & 7
    full = []
    for k in range(MOMENTS):
        diag = [lane_bc(packed, s * MOMENTS + k) for s in range(SHIFTS)]
        x = diag[0]
        for s in range(1, SHIFTS):
            x = jnp.where(gap == s, diag[s], x)
        for s in range(1, 4):
            x = jnp.where(gap == 8 - s, pltpu.roll(diag[s], 8 - s, 0), x)
        full.append(x)
    block = lane >> 3
    T = []
    for m in range(S):
        x = full[9 + m] * (1.0 / SHIFT)
        for n in range(S):
            x = jnp.where(block == n, full[m + n], x)
        T.append(x)
    for kb in range(S):
        base = 8 * kb
        cols = {m: [lane_bc(T[m], base + j) for j in range(8)] for m in range(S)}
        piv = list(cols[kb])
        g = T[kb]
        for k in range(8):
            inv = 1.0 / row_bc(piv[k], k)
            here = sub == k
            for j in range(k + 1, 8):
                r = row_bc(piv[j], k) * inv
                piv[j] = jnp.where(here, r, piv[j] - piv[k] * r)
            r = row_bc(g, k) * inv
            g = jnp.where(here, r, g - piv[k] * r)
        q = [row_bc(g, a) for a in range(8)]
        for m in range(S):
            if m == kb:
                T[m] = g
                continue
            s0 = cols[m][0] * q[0]
            s1 = cols[m][1] * q[1]
            for a in range(2, 8, 2):
                s0 = s0 + cols[m][a] * q[a]
                s1 = s1 + cols[m][a + 1] * q[a + 1]
            T[m] = T[m] - (s0 + s1)
    return T


def spread(T, W):
    sub = lax.broadcasted_iota(jnp.int32, (8, LANES), 0)
    for m in range(S):
        cols = [lane_bc(T[m], 8 * S + k) for k in range(8)]
        for s in range(8):
            x = cols[0]
            for k in range(1, 8):
                x = jnp.where(((sub - s) & 7) == k, cols[k], x)
            W[8 * m + s] = x


def combine(V, W, X, first, rows, width):
    w = [W[j] for j in range(8 * S)]

    def row(i, c):
        for t in range(width // LANES):
            sl = pl.ds(LANES * t, LANES)
            b = [V[m, i, :, sl] for m in range(S)]
            out = None
            for s in range(8):
                z = b[0] * w[s]
                for m in range(1, S):
                    z = z + b[m] * w[8 * m + s]
                if s:
                    z = pltpu.roll(z, 8 - s, 0)
                out = z if out is None else out + z
            X[i, :, sl] = out
        return c

    lax.fori_loop(first, first + rows, row, 0)


def kernel(
    nr, nc, rhs, ecls, lcls, via, table, xo, ro,
    V, E, L, C, X1, X2, ELP, RE, RW, CE, CW, RB, W, hs, hr, rs, rr,
):
    rows, own = rhs.shape[1], rhs.shape[2]
    ext = rows + 2 * D
    width = own + LANES
    me_r = lax.axis_index("rows")
    me_c = lax.axis_index("cols")
    up, down = (me_r + nr - 1) % nr, (me_r + 1) % nr
    west, east = (me_c + nc - 1) % nc, (me_c + 1) % nc

    barrier = pltpu.get_barrier_semaphore()

    def greet(r, c):
        pl.semaphore_signal(barrier, inc=1, device_id=(r, c), device_id_type=MESH)

    for r in (up, down):
        for c in (west, east):
            greet(r, c)
    for d in range(1, nc):
        greet(me_r, (me_c + d) % nc)
    for d in range(1, nr):
        greet((me_r + d) % nr, me_c)

    for g in range(rows // 8):
        for t in range(own // LANES):
            rsl, sl = pl.ds(8 * g, 8), pl.ds(LANES * t, LANES)
            row_id = lax.broadcasted_iota(jnp.int32, (8, LANES), 0) + (me_r * rows + 8 * g)
            col_id = lax.broadcasted_iota(jnp.int32, (8, LANES), 1) + (me_c * own + LANES * t)
            ec, lc = ecls[rsl, sl], lcls[rsl, sl]
            e = jnp.zeros((8, LANES), f32)
            l = jnp.zeros((8, LANES), f32)
            for k in range(table.shape[0]):
                e = jnp.where(ec == k, table[k], e)
                l = jnp.where(lc == k, table[k], l)
            at = pl.ds(CH + 8 * g, 8)
            ELP[0, at, sl] = jnp.where(col_id < nc * own - 1, e, 0.0)
            ELP[1, at, sl] = jnp.where(row_id < nr * rows - 1, l, 0.0)
            ELP[2, at, sl] = PAD_G * via[rsl, sl].astype(f32)
            V[0, pl.ds(D + 8 * g, 8), :, sl] = jnp.swapaxes(rhs[:, rsl, sl], 0, 1)

    pl.semaphore_wait(barrier, nr + nc + 2)

    copies = []

    def send(src, dst, r, c):
        n = len(copies)
        copy = pltpu.make_async_remote_copy(
            src_ref=src, dst_ref=dst, send_sem=hs.at[n], recv_sem=hr.at[n],
            device_id=(r, c), device_id_type=MESH,
        )
        copy.start()
        copies.append(copy)

    top, bottom = pl.ds(D, D), pl.ds(rows, D)
    after, before = pl.ds(D + rows, D), pl.ds(0, D)
    inner = pl.ds(D, rows)
    body = pl.ds(0, own)
    lo, hi = pl.ds(0, LANES), pl.ds(own - LANES, LANES)
    send(V.at[0, top, :, body], V.at[0, after, :, body], up, me_c)
    send(V.at[0, bottom, :, body], V.at[0, before, :, body], down, me_c)
    send(V.at[0, inner, :, lo], RE.at[inner], me_r, west)
    send(V.at[0, inner, :, hi], RW.at[inner], me_r, east)
    send(V.at[0, top, :, lo], RE.at[after], up, west)
    send(V.at[0, bottom, :, lo], RE.at[before], down, west)
    send(V.at[0, top, :, hi], RW.at[after], up, east)
    send(V.at[0, bottom, :, hi], RW.at[before], down, east)
    ctop, cbottom = pl.ds(CH, CH), pl.ds(rows, CH)
    cafter, cbefore = pl.ds(CH + rows, CH), pl.ds(0, CH)
    cinner = pl.ds(CH, rows)
    send(ELP.at[:, ctop, body], ELP.at[:, cafter, body], up, me_c)
    send(ELP.at[:, cbottom, body], ELP.at[:, cbefore, body], down, me_c)
    send(ELP.at[:, cinner, lo], CE.at[:, cinner], me_r, west)
    send(ELP.at[:, cinner, hi], CW.at[:, cinner], me_r, east)
    send(ELP.at[:, ctop, lo], CE.at[:, cafter], up, west)
    send(ELP.at[:, cbottom, lo], CE.at[:, cbefore], down, west)
    send(ELP.at[:, ctop, hi], CW.at[:, cafter], up, east)
    send(ELP.at[:, cbottom, hi], CW.at[:, cbefore], down, east)
    for copy in copies:
        copy.wait_recv()
    for copy in copies:
        copy.wait_send()

    lane = lax.broadcasted_iota(jnp.int32, (8, LANES), 1)
    side = pl.ds(own, LANES)

    def side_row(i, c):
        V[0, i, :, side] = jnp.where(lane < LANES // 2, RE[i], RW[i])
        return c

    lax.fori_loop(0, ext, side_row, 0, unroll=4)
    crows = rows + 2 * CH
    for p in range(3):
        for g in range(crows // 8):
            at = pl.ds(8 * g, 8)
            ELP[p, at, side] = jnp.where(lane < LANES // 2, CE[p, at], CW[p, at])
    e, l = ELP[0], ELP[1]
    scale = 1.0 / SHIFT
    around = e + pltpu.roll(e, 1, 1) + l + pltpu.roll(l, 1, 0)
    ELP[2] = (around + (ELP[2] + LEAK)) * scale - 1.0
    ELP[0] = e * scale
    ELP[1] = l * scale

    def expand(i, c):
        for p, ref in enumerate((E, L, C)):
            ref[i] = jnp.broadcast_to(ELP[p, pl.ds(i + (CH - D), 1), :], (8, width))
        return c

    lax.fori_loop(0, ext, expand, 0, unroll=2)

    def allsum(phase, tile, me, n, device):
        RB[phase, me] = tile

        def put(d, c):
            pltpu.make_async_remote_copy(
                src_ref=RB.at[phase, me], dst_ref=RB.at[phase, me],
                send_sem=rs.at[phase], recv_sem=rr.at[phase],
                device_id=device((me + d) % n), device_id_type=MESH,
            ).start()
            return c

        lax.fori_loop(1, n, put, 0)
        pending(phase, n).wait_recv()
        parts = [RB[phase, d] for d in range(n)]
        while len(parts) > 1:
            odd = parts[len(parts) // 2 * 2 :]
            parts = [parts[j] + parts[j + 1] for j in range(0, len(parts) - 1, 2)] + odd
        return parts[0]

    def pending(phase, n):
        some = RB.at[phase, pl.ds(0, n - 1)]
        return pltpu.make_async_remote_copy(
            src_ref=some, dst_ref=some, send_sem=rs.at[phase], recv_sem=rr.at[phase],
            device_id=(up, me_c), device_id_type=MESH,
        )

    for sweep in range(OUTER):
        depth = S * (OUTER - sweep)
        a = D - depth + 1
        count = rows + 2 * depth - 2

        def level(m, c):
            stencil_rows(V.at[m], V.at[m + 1], E, L, C, a, count)
            return c

        lax.fori_loop(0, S, level, 0)
        tile = moments(V, D, rows, own)
        tile = allsum(2 * sweep, tile, me_c, nc, lambda c: (me_r, c))
        tile = allsum(2 * sweep + 1, tile, me_r, nr, lambda r: (r, me_c))
        spread(solve(tile), W)
        X = (X1, X2)[sweep]
        depth -= S
        combine(V, W, X, D - depth - 1, rows + 2 * depth + 2, width)
        stencil_rows(X, V.at[1], E, L, C, D - depth, rows + 2 * depth)

        def update(i, c):
            V[0, i] = V[0, i] - SHIFT * (V[1, i] + X[i])
            return c

        lax.fori_loop(D - depth, D + rows + depth, update, 0, unroll=2)

    for g in range(rows // 8):
        for t in range(own // LANES):
            rsl, sl = pl.ds(8 * g, 8), pl.ds(LANES * t, LANES)
            at = pl.ds(D + 8 * g, 8)
            xo[:, rsl, sl] = jnp.swapaxes(X1[at, :, sl] + X2[at, :, sl], 0, 1)
            ro[:, rsl, sl] = jnp.swapaxes(V[0, at, :, sl], 0, 1)
    for phase in range(2 * OUTER):
        pending(phase, (nc, nr)[phase % 2]).wait_send()


def local(right_side, east_class, lower_class, via_mask, class_conductance):
    nr, nc = lax.axis_size("rows"), lax.axis_size("cols")
    loads, rows, own = right_side.shape
    ext, width, crows = rows + 2 * D, own + LANES, rows + 2 * CH
    vmem = pl.BlockSpec(memory_space=pltpu.VMEM)
    field = pltpu.VMEM((ext, loads, width), f32)
    return pl.pallas_call(
        functools.partial(kernel, nr, nc),
        out_shape=[jax.ShapeDtypeStruct(right_side.shape, f32)] * 2,
        in_specs=[vmem] * 4 + [pl.BlockSpec(memory_space=pltpu.SMEM)],
        out_specs=[vmem] * 2,
        scratch_shapes=[
            pltpu.VMEM((S + 1, ext, loads, width), f32),
            field, field, field, field, field,
            pltpu.VMEM((3, crows, width), f32),
            pltpu.VMEM((ext, loads, LANES), f32),
            pltpu.VMEM((ext, loads, LANES), f32),
            pltpu.VMEM((3, crows, LANES), f32),
            pltpu.VMEM((3, crows, LANES), f32),
            pltpu.VMEM((2 * OUTER, max(nr, nc), 8, LANES), f32),
            pltpu.VMEM((8 * S, 8, LANES), f32),
            pltpu.SemaphoreType.DMA((16,)),
            pltpu.SemaphoreType.DMA((16,)),
            pltpu.SemaphoreType.DMA((2 * OUTER,)),
            pltpu.SemaphoreType.DMA((2 * OUTER,)),
        ],
        compiler_params=pltpu.CompilerParams(
            collective_id=0, has_side_effects=True, vmem_limit_bytes=40 * 2**20
        ),
    )(right_side, east_class, lower_class, via_mask, class_conductance)


def solution(mesh):
    return jax.shard_map(
        local,
        mesh=mesh,
        in_specs=(
            P(None, "rows", "cols"),
            P("rows", "cols"),
            P("rows", "cols"),
            P("rows", "cols"),
            P(),
        ),
        out_specs=(P(None, "rows", "cols"), P(None, "rows", "cols")),
        check_vma=False,
    )
```

```python
import functools

import jax
import jax.numpy as jnp
from jax import lax
from jax.experimental import pallas as pl
from jax.experimental.pallas import tpu as pltpu
from jax.sharding import PartitionSpec as P

S = 5
OUTER = 2
D = S * OUTER
LEAK = 0.05
PAD_G = 2.0
SHIFT = 6.0
LANES = 128
CH = 16
f32 = jnp.float32
bf16 = jnp.bfloat16
MESH = pl.DeviceIdType.MESH


def lane_bc(x, lane):
    return jnp.broadcast_to(x[:, lane : lane + 1], x.shape)


def row_bc(x, row):
    return jnp.broadcast_to(x[row : row + 1, :], x.shape)


def stencil_rows(src, E, L, C, first, count, put):
    width = src.shape[-1]
    below = L[first - 1] * src[first - 1]
    for q in range(count):
        i = first + q
        v = src[i]
        e = E[i]
        l = L[i]
        put(
            i,
            (C[i] * v - e * pltpu.roll(v, width - 1, 1))
            - (pltpu.roll(e * v, 1, 1) + (l * src[i + 1] + below)),
        )
        below = l * v


def halves(x):
    high = x.astype(bf16)
    low = (x - high.astype(f32)).astype(bf16)
    return jnp.concatenate([high, low], 0)


def moments(V, VB, first, rows, own, step=8):
    def some(j, acc):
        left, right = [], []
        for q in range(step):
            i = first + j * step + q
            b = [V[m, i] for m in range(S + 1)]
            split = halves(jnp.concatenate(b[:S], 0))
            VB[i] = split
            left.append(split[:, :own])
            right.append(
                halves(jnp.concatenate([(b[m] + b[m + 1])[:, :own] for m in range(S)] + [b[0][:, :own]], 0))
            )
        return acc + lax.dot_general(
            jnp.concatenate(left, 1), jnp.concatenate(right, 1),
            (((1,), (1,)), ((), ())), preferred_element_type=f32,
        )

    n, k = 8 * S, 8 * (S + 1)
    acc = lax.fori_loop(0, rows // step, some, jnp.zeros((2 * n, 2 * k), f32))
    gram = (acc[:n, :k] + acc[n:, k:]) + (acc[:n, k:] + acc[n:, :k])
    gram = jnp.concatenate([gram, jnp.zeros((n, LANES - k), f32)], 1)
    block = lax.broadcasted_iota(jnp.int32, (8, LANES), 1) >> 3
    out = jnp.zeros((8, LANES), f32)
    for m in range(S):
        x = gram[8 * m : 8 * m + 8]
        out = jnp.where((block >> 1) == m, x if m == 0 else pltpu.roll(x, 8 * m, 1), out)
    for m in range(S):
        x = pltpu.roll(gram[8 * m : 8 * m + 8], 32 + 8 * m, 1)
        out = jnp.where(block == 9 + m, x, out)
    return out


def solve(packed):
    lane = lax.broadcasted_iota(jnp.int32, (8, LANES), 1)
    sub = lax.broadcasted_iota(jnp.int32, (8, LANES), 0)
    T = [packed if m == 0 else pltpu.roll(packed, LANES - 8 * m, 1) for m in range(S)]
    T.append(pltpu.roll(packed, LANES - 72, 1) * (1.0 / SHIFT))
    for kb in range(S):
        base = 8 * kb
        cols = {m: [lane_bc(T[m], base + j) for j in range(8)] for m in range(kb, S + 1)}
        piv = list(cols[kb])
        within = (lane >= base) & (lane < base + 8)
        g = jnp.where(within, jnp.where(lane - base == sub, -1.0, 0.0), T[kb])
        for k in range(8):
            inv = 1.0 / row_bc(piv[k], k)
            here = sub == k
            for j in range(k + 1, 8):
                r = row_bc(piv[j], k) * inv
                piv[j] = jnp.where(here, r, piv[j] - piv[k] * r)
            r = row_bc(g, k) * inv
            g = jnp.where(here, r, g - piv[k] * r)
        q = [row_bc(g, a) for a in range(8)]
        for m in range(kb + 1, S + 1):
            s0 = cols[m][0] * q[0]
            s1 = cols[m][1] * q[1]
            for a in range(2, 8, 2):
                s0 = s0 + cols[m][a] * q[a]
                s1 = s1 + cols[m][a + 1] * q[a + 1]
            T[m] = jnp.where(within, 0.0, T[m]) - (s0 + s1)
    return T[S]


def combine(VB, coefficients, X, first, rows, step):
    lane = lax.broadcasted_iota(jnp.int32, (8, LANES), 1)
    n = 8 * S
    twice = jnp.where(lane < n, coefficients, pltpu.roll(coefficients, n, 1))
    left = halves(twice)[:, : 2 * n]

    def some(j, c):
        for q in range(step):
            i = first + j * step + q
            out = lax.dot_general(
                left, VB[i], (((1,), (0,)), ((), ())), preferred_element_type=f32
            )
            X[i] = out[:8] + out[8:]
        return c

    lax.fori_loop(0, rows // step, some, 0)


def kernel(
    nr, nc, rhs_in, ecls_in, lcls_in, via_in, table_in, xo, ro,
    rhs, ecls, lcls, via, table,
    V, VB, E, L, C, X1, X2, ELP, CP, RE, RW, CE, CW, CS, CR, RB, ls, hs, hr, rs, rr,
):
    rows, own = rhs.shape[1], rhs.shape[2]
    ext = rows + 2 * D
    width = own + LANES
    me_r = lax.axis_index("rows")
    me_c = lax.axis_index("cols")
    up, down = (me_r + nr - 1) % nr, (me_r + 1) % nr
    west, east = (me_c + nc - 1) % nc, (me_c + 1) % nc

    loads = []
    for j, (src, dst) in enumerate(
        ((rhs_in, rhs), (ecls_in, ecls), (lcls_in, lcls), (via_in, via), (table_in, table))
    ):
        loads.append(pltpu.make_async_copy(src, dst, ls.at[j]))
        loads[-1].start()

    barrier = pltpu.get_barrier_semaphore()

    def greet(r, c):
        pl.semaphore_signal(barrier, inc=1, device_id=(r, c), device_id_type=MESH)

    for r in (up, down):
        for c in (west, east):
            greet(r, c)
    for d in range(1, nc):
        greet(me_r, (me_c + d) % nc)
    for d in range(1, nr):
        greet((me_r + d) % nr, me_c)

    copies = [None] * 16

    def send(n, src, dst, r, c):
        copies[n] = pltpu.make_async_remote_copy(
            src_ref=src, dst_ref=dst, send_sem=hs.at[n], recv_sem=hr.at[n],
            device_id=(r, c), device_id_type=MESH,
        )
        copies[n].start()

    lane = lax.broadcasted_iota(jnp.int32, (8, LANES), 1)
    tiles = [(8 * g, LANES * t) for g in range(rows // 8) for t in range(own // LANES)]
    loads[0].wait()
    for r0, c0 in tiles:
        V[0, pl.ds(D + r0, 8), :, pl.ds(c0, LANES)] = jnp.swapaxes(
            rhs[:, pl.ds(r0, 8), pl.ds(c0, LANES)], 0, 1
        )

    pl.semaphore_wait(barrier, nr + nc + 2)

    body = pl.ds(0, own)
    lo, hi = pl.ds(0, LANES), pl.ds(own - LANES, LANES)
    inner = pl.ds(D, rows)
    send(0, V.at[0, pl.ds(D, S), :, body], V.at[0, pl.ds(D + rows, S), :, body], up, me_c)
    send(1, V.at[0, pl.ds(D + rows - S, S), :, body], V.at[0, pl.ds(D - S, S), :, body], down, me_c)
    send(2, V.at[0, inner, :, lo], RE, me_r, west)
    send(3, V.at[0, inner, :, hi], RW, me_r, east)

    for load in loads[1:]:
        load.wait()
    for r0, c0 in tiles:
        rsl, sl = pl.ds(r0, 8), pl.ds(c0, LANES)
        row_id = lax.broadcasted_iota(jnp.int32, (8, LANES), 0) + (me_r * rows + r0)
        col_id = lane + (me_c * own + c0)
        ec, lc = ecls[rsl, sl], lcls[rsl, sl]
        e = jnp.zeros((8, LANES), f32)
        l = jnp.zeros((8, LANES), f32)
        for k in range(table.shape[0]):
            e = jnp.where(ec == k, table[k], e)
            l = jnp.where(lc == k, table[k], l)
        at = pl.ds(CH + r0, 8)
        ELP[0, at, sl] = jnp.where(col_id < nc * own - 1, e, 0.0)
        ELP[1, at, sl] = jnp.where(row_id < nr * rows - 1, l, 0.0)
        ELP[2, at, sl] = PAD_G * via[rsl, sl].astype(f32)
    cinner = pl.ds(CH, rows)
    send(4, ELP.at[:, pl.ds(CH, 8), body], ELP.at[:, pl.ds(CH + rows, 8), body], up, me_c)
    send(5, ELP.at[:, pl.ds(CH + rows - 8, 8), body], ELP.at[:, pl.ds(CH - 8, 8), body], down, me_c)
    send(6, ELP.at[:, cinner, lo], CE, me_r, west)
    send(7, ELP.at[:, cinner, hi], CW, me_r, east)
    for n, (bottom, right) in enumerate(((0, 0), (0, 1), (1, 0), (1, 1))):
        sl = hi if right else lo
        x = jnp.zeros((8, LANES), f32)
        for j in range(D):
            i = (rows if bottom else D) + j
            x = jnp.where(lane >= 12 * j, pltpu.roll(V[0, i, :, sl], (12 * j + 10 * right) % LANES, 1), x)
        CS[n, 0] = x
        x = jnp.zeros((8, LANES), f32)
        for j in range(6):
            i = (rows if bottom else CH) + 8 * (j % 2)
            x = jnp.where(
                lane >= 16 * j, pltpu.roll(ELP[j // 2, pl.ds(i, 8), sl], (16 * j + 16 * right) % LANES, 1), x
            )
        CS[n, 1] = x
        send(8 + n, CS.at[n], CR.at[n], down if bottom else up, east if right else west)
    send(12, V.at[0, pl.ds(D + S, S), :, body], V.at[0, pl.ds(D + rows + S, S), :, body], up, me_c)
    send(13, V.at[0, pl.ds(rows, S), :, body], V.at[0, pl.ds(0, S), :, body], down, me_c)
    send(14, ELP.at[:, pl.ds(CH + 8, 8), body], ELP.at[:, pl.ds(CH + rows + 8, 8), body], up, me_c)
    send(15, ELP.at[:, pl.ds(rows, 8), body], ELP.at[:, pl.ds(0, 8), body], down, me_c)

    scale = 1.0 / SHIFT
    side = pl.ds(own, LANES)
    everywhere = pl.ds(0, width)

    def expand(first, count, sl, planes):
        for i in range(first, first + count):
            for p in planes:
                at = pl.ds(i + CH - D, 1)
                x = ELP[p, at, sl] * scale if p < 2 else CP[at, sl]
                (E, L, C)[p][i, :, sl] = jnp.broadcast_to(x, (8, sl.size))

    expand(D, rows, body, (0, 1))
    for n in range(12):
        copies[n].wait_recv()

    left = lane < LANES // 2

    def side_row(i, c):
        V[0, i, :, side] = jnp.where(left, RE[i - D], RW[i - D])
        return c

    lax.fori_loop(D, D + rows, side_row, 0, unroll=4)
    for bottom in range(2):
        a, b = 2 - 2 * bottom, 3 - 2 * bottom
        for j in range(D):
            i = (D + rows if bottom else 0) + j
            V[0, i, :, side] = jnp.where(
                left,
                pltpu.roll(CR[a, 0], (LANES - 12 * j) % LANES, 1),
                pltpu.roll(CR[b, 0], (LANES - 10 - 12 * j) % LANES, 1),
            )
        for j in range(6):
            at = pl.ds((CH + rows if bottom else 0) + 8 * (j % 2), 8)
            ELP[j // 2, at, side] = jnp.where(
                left,
                pltpu.roll(CR[a, 1], (LANES - 16 * j) % LANES, 1),
                pltpu.roll(CR[b, 1], (LANES - 16 - 16 * j) % LANES, 1),
            )
    for p in range(3):
        for r0 in range(0, rows, 8):
            at = pl.ds(r0, 8)
            ELP[p, pl.ds(CH + r0, 8), side] = jnp.where(left, CE[p, at], CW[p, at])

    def centre(first, count):
        at = pl.ds(first, count)
        e, l = ELP[0, at], ELP[1, at]
        around = (e + pltpu.roll(e, 1, 1)) + (l + pltpu.roll(l, 1, 0))
        CP[at] = (around + (ELP[2, at] + LEAK)) * scale - 1.0

    centre(CH - 8, rows + 16)
    expand(D - S, S, everywhere, (0, 1))
    expand(D + rows, S, everywhere, (0, 1))
    expand(D, rows, side, (0, 1))
    expand(D - S, rows + 2 * S, everywhere, (2,))

    def allsum(phase, tile, me, n, device, meanwhile):
        RB[phase, me] = tile
        for d in range(1, n):
            pltpu.make_async_remote_copy(
                src_ref=RB.at[phase, me], dst_ref=RB.at[phase, me],
                send_sem=rs.at[phase], recv_sem=rr.at[phase],
                device_id=device((me + d) % n), device_id_type=MESH,
            ).start()
        meanwhile()
        pending(phase, n).wait_recv()
        parts = [RB[phase, d] for d in range(n)]
        while len(parts) > 1:
            odd = parts[len(parts) // 2 * 2 :]
            parts = [parts[j] + parts[j + 1] for j in range(0, len(parts) - 1, 2)] + odd
        return parts[0]

    def pending(phase, n):
        some = RB.at[phase, pl.ds(0, n - 1)]
        return pltpu.make_async_remote_copy(
            src_ref=some, dst_ref=some, send_sem=rs.at[phase], recv_sem=rr.at[phase],
            device_id=(up, me_c), device_id_type=MESH,
        )

    def cast(first, count):
        for i in range(first, first + count):
            VB[i] = halves(jnp.concatenate([V[m, i] for m in range(S)], 0))

    def store(ref):
        def put(i, x):
            ref[i] = x

        return put

    def outer_rows():
        for n in range(12, 16):
            copies[n].wait_recv()
        centre(0, 16)
        centre(CH + rows, 16)
        expand(0, S + 1, everywhere, (0, 1, 2))
        expand(ext - S - 1, S + 1, everywhere, (0, 1, 2))
        for m in range(S - 1):
            stencil_rows(V.at[m], E, L, C, m + 1, S, store(V.at[m + 1]))
            stencil_rows(V.at[m], E, L, C, ext - S - 1 - m, S, store(V.at[m + 1]))

    def outer_cast(depth):
        cast(D - depth, depth)
        cast(D + rows, depth)

    for sweep in range(OUTER):

        def level(m, c):
            stencil_rows(V.at[m], E, L, C, D - S + 1, rows + 2 * S - 2, store(V.at[m + 1]))
            return c

        lax.fori_loop(0, S, level, 0)
        depth = S * (OUTER - 1 - sweep)
        tile = moments(V, VB, D, rows, own)
        tile = allsum(
            2 * sweep, tile, me_c, nc, lambda c: (me_r, c),
            outer_rows if sweep == 0 else lambda: outer_cast(depth + 1),
        )
        tile = allsum(
            2 * sweep + 1, tile, me_r, nr, lambda r: (r, me_c),
            (lambda: outer_cast(depth + 1)) if sweep == 0 else lambda: None,
        )
        if sweep == 0:
            for copy in copies:
                copy.wait_send()
        X = (X1, X2)[sweep]
        count = rows + 2 * depth + 2
        combine(VB, solve(tile), X, D - depth - 1, count, 11 if count % 11 == 0 else 17)

        def update(i, x):
            V[0, i] = V[0, i] - SHIFT * (x + X[i])

        stencil_rows(X, E, L, C, D - depth, rows + 2 * depth, update)

    for r0, c0 in tiles:
        rsl, sl = pl.ds(r0, 8), pl.ds(c0, LANES)
        at = pl.ds(D + r0, 8)
        xo[:, rsl, sl] = jnp.swapaxes(X1[at, :, sl] + X2[at, :, sl], 0, 1)
        ro[:, rsl, sl] = jnp.swapaxes(V[0, at, :, sl], 0, 1)
    for phase in range(2 * OUTER):
        pending(phase, (nc, nr)[phase % 2]).wait_send()


def local(right_side, east_class, lower_class, via_mask, class_conductance):
    nr, nc = lax.axis_size("rows"), lax.axis_size("cols")
    loads, rows, own = right_side.shape
    ext, width, crows = rows + 2 * D, own + LANES, rows + 2 * CH
    vmem = pl.BlockSpec(memory_space=pltpu.VMEM)
    field = pltpu.VMEM((ext, loads, width), f32)
    dma = pltpu.SemaphoreType.DMA
    return pl.pallas_call(
        functools.partial(kernel, nr, nc),
        out_shape=[jax.ShapeDtypeStruct(right_side.shape, f32)] * 2,
        in_specs=[pl.BlockSpec(memory_space=pltpu.HBM)] * 5,
        out_specs=[vmem] * 2,
        scratch_shapes=[
            pltpu.VMEM(right_side.shape, f32),
            pltpu.VMEM((rows, own), jnp.int32),
            pltpu.VMEM((rows, own), jnp.int32),
            pltpu.VMEM((rows, own), jnp.int32),
            pltpu.SMEM(class_conductance.shape, f32),
            pltpu.VMEM((S + 1, ext, loads, width), f32),
            pltpu.VMEM((ext, 2 * loads * S, width), bf16),
            field, field, field, field, field,
            pltpu.VMEM((3, crows, width), f32),
            pltpu.VMEM((crows, width), f32),
            pltpu.VMEM((rows, loads, LANES), f32),
            pltpu.VMEM((rows, loads, LANES), f32),
            pltpu.VMEM((3, rows, LANES), f32),
            pltpu.VMEM((3, rows, LANES), f32),
            pltpu.VMEM((4, 2, 8, LANES), f32),
            pltpu.VMEM((4, 2, 8, LANES), f32),
            pltpu.VMEM((2 * OUTER, max(nr, nc), 8, LANES), f32),
            dma((5,)),
            dma((16,)),
            dma((16,)),
            dma((2 * OUTER,)),
            dma((2 * OUTER,)),
        ],
        compiler_params=pltpu.CompilerParams(
            collective_id=0, has_side_effects=True, vmem_limit_bytes=40 * 2**20
        ),
    )(right_side, east_class, lower_class, via_mask, class_conductance)


def solution(mesh):
    return jax.shard_map(
        local,
        mesh=mesh,
        in_specs=(
            P(None, "rows", "cols"),
            P("rows", "cols"),
            P("rows", "cols"),
            P("rows", "cols"),
            P(),
        ),
        out_specs=(P(None, "rows", "cols"), P(None, "rows", "cols")),
        check_vma=False,
    )
```

```python
import functools

import jax
import jax.numpy as jnp
from jax import lax
from jax.experimental import pallas as pl
from jax.experimental.pallas import tpu as pltpu
from jax.sharding import PartitionSpec as P

S = 5
OUTER = 2
D = S * OUTER
LEAK = 0.05
PAD_G = 2.0
SHIFT = 6.0
LANES = 128
CH = 16
f32 = jnp.float32
bf16 = jnp.bfloat16
MESH = pl.DeviceIdType.MESH


def lane_bc(x, lane):
    return jnp.broadcast_to(x[:, lane : lane + 1], x.shape)


def row_bc(x, row):
    return jnp.broadcast_to(x[row : row + 1, :], x.shape)


def stencil_rows(src, E, L, C, first, count, put):
    width = src.shape[-1]
    below = L[first - 1] * src[first - 1]
    for q in range(count):
        i = first + q
        v = src[i]
        e = E[i]
        l = L[i]
        put(
            i,
            (C[i] * v - e * pltpu.roll(v, width - 1, 1))
            - (pltpu.roll(e * v, 1, 1) + (l * src[i + 1] + below)),
        )
        below = l * v


def halves(x):
    high = x.astype(bf16)
    low = (x - high.astype(f32)).astype(bf16)
    return jnp.concatenate([high, low], 0)


def products(V, VB, lines, own):
    left, right = [], []
    for i in lines:
        b = [V[m, i] for m in range(S + 1)]
        split = halves(jnp.concatenate(b[:S], 0))
        VB[i] = split
        left.append(split[:, :own])
        right.append(
            halves(jnp.concatenate([(b[m] + b[m + 1])[:, :own] for m in range(S)] + [b[0][:, :own]], 0))
        )
    return lax.dot_general(
        jnp.concatenate(left, 1), jnp.concatenate(right, 1),
        (((1,), (1,)), ((), ())), preferred_element_type=f32,
    )


def product_blocks(V, VB, first, blocks, step, own):
    def some(j, acc):
        return acc + products(V, VB, [first + j * step + q for q in range(step)], own)

    return lax.fori_loop(0, blocks, some, jnp.zeros((16 * S, 16 * (S + 1)), f32))


def moments(acc):
    n, k = 8 * S, 8 * (S + 1)
    gram = (acc[:n, :k] + acc[n:, k:]) + (acc[:n, k:] + acc[n:, :k])
    gram = jnp.concatenate([gram, jnp.zeros((n, LANES - k), f32)], 1)
    block = lax.broadcasted_iota(jnp.int32, (8, LANES), 1) >> 3
    out = jnp.zeros((8, LANES), f32)
    for m in range(S):
        x = gram[8 * m : 8 * m + 8]
        out = jnp.where((block >> 1) == m, x if m == 0 else pltpu.roll(x, 8 * m, 1), out)
    for m in range(S):
        x = pltpu.roll(gram[8 * m : 8 * m + 8], 32 + 8 * m, 1)
        out = jnp.where(block == 9 + m, x, out)
    return out


def solve(packed):
    lane = lax.broadcasted_iota(jnp.int32, (8, LANES), 1)
    sub = lax.broadcasted_iota(jnp.int32, (8, LANES), 0)
    T = [packed if m == 0 else pltpu.roll(packed, LANES - 8 * m, 1) for m in range(S)]
    T.append(pltpu.roll(packed, LANES - 72, 1) * (1.0 / SHIFT))
    for kb in range(S):
        base = 8 * kb
        cols = {m: [lane_bc(T[m], base + j) for j in range(8)] for m in range(kb, S + 1)}
        piv = list(cols[kb])
        within = (lane >= base) & (lane < base + 8)
        g = jnp.where(within, jnp.where(lane - base == sub, -1.0, 0.0), T[kb])
        for k in range(8):
            inv = 1.0 / row_bc(piv[k], k)
            here = sub == k
            for j in range(k + 1, 8):
                r = row_bc(piv[j], k) * inv
                piv[j] = jnp.where(here, r, piv[j] - piv[k] * r)
            r = row_bc(g, k) * inv
            g = jnp.where(here, r, g - piv[k] * r)
        q = [row_bc(g, a) for a in range(8)]
        for m in range(kb + 1, S + 1):
            s0 = cols[m][0] * q[0]
            s1 = cols[m][1] * q[1]
            for a in range(2, 8, 2):
                s0 = s0 + cols[m][a] * q[a]
                s1 = s1 + cols[m][a + 1] * q[a + 1]
            T[m] = jnp.where(within, 0.0, T[m]) - (s0 + s1)
    return T[S]


def combine(VB, coefficients, X, first, rows, step):
    lane = lax.broadcasted_iota(jnp.int32, (8, LANES), 1)
    n = 8 * S
    twice = jnp.where(lane < n, coefficients, pltpu.roll(coefficients, n, 1))
    left = halves(twice)[:, : 2 * n]

    def some(j, c):
        for q in range(step):
            i = first + j * step + q
            out = lax.dot_general(
                left, VB[i], (((1,), (0,)), ((), ())), preferred_element_type=f32
            )
            X[i] = out[:8] + out[8:]
        return c

    lax.fori_loop(0, rows // step, some, 0)


def kernel(
    nr, nc, rhs_in, ecls_in, lcls_in, via_in, table_in, xo, ro,
    rhs, ecls, lcls, via, table,
    V, VB, E, L, C, X1, X2, ELP, CP, PS, PR, CS, CR, RB, ls, hs, hr, rs, rr,
):
    rows, own = rhs.shape[1], rhs.shape[2]
    ext = rows + 2 * D
    width = own + LANES
    me_r = lax.axis_index("rows")
    me_c = lax.axis_index("cols")
    up, down = (me_r + nr - 1) % nr, (me_r + 1) % nr
    west, east = (me_c + nc - 1) % nc, (me_c + 1) % nc

    loads = []
    for j, (src, dst) in enumerate(
        ((rhs_in, rhs), (ecls_in, ecls), (lcls_in, lcls), (via_in, via), (table_in, table))
    ):
        loads.append(pltpu.make_async_copy(src, dst, ls.at[j]))
        loads[-1].start()

    barrier = pltpu.get_barrier_semaphore()

    def greet(r, c):
        pl.semaphore_signal(barrier, inc=1, device_id=(r, c), device_id_type=MESH)

    for r in (up, down):
        for c in (west, east):
            greet(r, c)
    for d in range(1, nc):
        greet(me_r, (me_c + d) % nc)
    for d in range(1, nr):
        greet((me_r + d) % nr, me_c)

    copies = [None] * 14

    def send(n, src, dst, r, c):
        copies[n] = pltpu.make_async_remote_copy(
            src_ref=src, dst_ref=dst, send_sem=hs.at[n], recv_sem=hr.at[n],
            device_id=(r, c), device_id_type=MESH,
        )
        copies[n].start()

    lane = lax.broadcasted_iota(jnp.int32, (8, LANES), 1)
    tiles = [(8 * g, LANES * t) for g in range(rows // 8) for t in range(own // LANES)]
    body = pl.ds(0, own)
    ends = (pl.ds(0, LANES), pl.ds(own - LANES, LANES))

    for load in loads[1:]:
        load.wait()
    for r0, c0 in tiles:
        rsl, sl = pl.ds(r0, 8), pl.ds(c0, LANES)
        row_id = lax.broadcasted_iota(jnp.int32, (8, LANES), 0) + (me_r * rows + r0)
        col_id = lane + (me_c * own + c0)
        ec, lc = ecls[rsl, sl], lcls[rsl, sl]
        e = jnp.zeros((8, LANES), f32)
        l = jnp.zeros((8, LANES), f32)
        for k in range(table.shape[0]):
            e = jnp.where(ec == k, table[k], e)
            l = jnp.where(lc == k, table[k], l)
        at = pl.ds(CH + r0, 8)
        ELP[0, at, sl] = jnp.where(col_id < nc * own - 1, e, 0.0)
        ELP[1, at, sl] = jnp.where(row_id < nr * rows - 1, l, 0.0)
        ELP[2, at, sl] = PAD_G * via[rsl, sl].astype(f32)
    loads[0].wait()
    for r0, c0 in tiles:
        V[0, pl.ds(D + r0, 8), :, pl.ds(c0, LANES)] = jnp.swapaxes(
            rhs[:, pl.ds(r0, 8), pl.ds(c0, LANES)], 0, 1
        )

    def pack(pieces, gap, skip):
        x = jnp.zeros((8, LANES), f32)
        for j, piece in enumerate(pieces):
            x = jnp.where(lane >= gap * j, pltpu.roll(piece, (gap * j + skip) % LANES, 1), x)
        return x

    ntile = rows // 8
    for right, sl in enumerate(ends):
        for g in range(ntile):
            PS[right, g] = pack([V[0, D + 8 * g + j, :, sl] for j in range(8)], 16, D * right)
        planes = [ELP[p, pl.ds(CH + 8 * g, 8), sl] for p in range(3) for g in range(ntile)]
        for q in range(0, len(planes), 8):
            PS[right, ntile + q // 8] = pack(planes[q : q + 8], 16, 16 * right)
        for bottom in range(2):
            n = 2 * bottom + right
            i, c = (rows, rows) if bottom else (D, CH)
            CS[n, 0] = pack([V[0, i + j, :, sl] for j in range(D)], 12, D * right)
            CS[n, 1] = pack(
                [ELP[j // 2, pl.ds(c + 8 * (j % 2), 8), sl] for j in range(6)], 16, 16 * right
            )

    pl.semaphore_wait(barrier, nr + nc + 2)

    send(0, V.at[0, pl.ds(D, S), :, body], V.at[0, pl.ds(D + rows, S), :, body], up, me_c)
    send(1, V.at[0, pl.ds(D + rows - S, S), :, body], V.at[0, pl.ds(D - S, S), :, body], down, me_c)
    send(2, PS.at[0], PR.at[0], me_r, west)
    send(3, PS.at[1], PR.at[1], me_r, east)
    send(4, ELP.at[:, pl.ds(CH, 8), body], ELP.at[:, pl.ds(CH + rows, 8), body], up, me_c)
    send(5, ELP.at[:, pl.ds(CH + rows - 8, 8), body], ELP.at[:, pl.ds(CH - 8, 8), body], down, me_c)
    for n in range(4):
        send(6 + n, CS.at[n], CR.at[n], down if n // 2 else up, east if n % 2 else west)
    send(10, V.at[0, pl.ds(D + S, S), :, body], V.at[0, pl.ds(D + rows + S, S), :, body], up, me_c)
    send(11, V.at[0, pl.ds(rows, S), :, body], V.at[0, pl.ds(0, S), :, body], down, me_c)
    send(12, ELP.at[:, pl.ds(CH + 8, 8), body], ELP.at[:, pl.ds(CH + rows + 8, 8), body], up, me_c)
    send(13, ELP.at[:, pl.ds(rows, 8), body], ELP.at[:, pl.ds(0, 8), body], down, me_c)

    scale = 1.0 / SHIFT
    side = pl.ds(own, LANES)
    everywhere = pl.ds(0, width)
    left = lane < LANES // 2

    def expand(first, count, sl, planes):
        for i in range(first, first + count):
            for p in planes:
                at = pl.ds(i + CH - D, 1)
                x = ELP[p, at, sl] * scale if p < 2 else CP[at, sl]
                (E, L, C)[p][i, :, sl] = jnp.broadcast_to(x, (8, sl.size))

    def centre(first, count):
        at = pl.ds(first, count)
        e, l = ELP[0, at], ELP[1, at]
        around = (e + pltpu.roll(e, 1, 1)) + (l + pltpu.roll(l, 1, 0))
        CP[at] = (around + (ELP[2, at] + LEAK)) * scale - 1.0

    def unpack(east_piece, west_piece, shift, wide):
        return jnp.where(
            left,
            pltpu.roll(east_piece, (LANES - shift) % LANES, 1),
            pltpu.roll(west_piece, (LANES - wide - shift) % LANES, 1),
        )

    def store(ref):
        def put(i, x):
            ref[i] = x

        return put

    def rim(m, outside):
        for first in (outside + m, ext - outside - m - S):
            stencil_rows(V.at[m], E, L, C, first, S, store(V.at[m + 1]))

    expand(D, rows, body, (0, 1))
    for n in (2, 3):
        copies[n].wait_recv()
    for i in range(rows):
        V[0, D + i, :, side] = unpack(PR[0, i // 8], PR[1, i // 8], 16 * (i % 8), D)
    for j in range(3 * ntile):
        q = ntile + j // 8
        ELP[j // ntile, pl.ds(CH + 8 * (j % ntile), 8), side] = unpack(
            PR[0, q], PR[1, q], 16 * (j % 8), 16
        )
    centre(CH, rows)
    expand(D, rows, side, (0, 1))
    expand(D + 1, rows - 1, everywhere, (2,))

    def inner_level(m, c):
        stencil_rows(V.at[m], E, L, C, D + 1, rows - 2, store(V.at[m + 1]))
        return c

    lax.fori_loop(0, S, inner_level, 0)
    gram = product_blocks(V, VB, D + S, 2, (rows - 2 * S) // 2, own)

    for n in (0, 1, 4, 5, 6, 7, 8, 9):
        copies[n].wait_recv()
    for bottom in range(2):
        a, b = 2 - 2 * bottom, 3 - 2 * bottom
        for j in range(D):
            V[0, (D + rows) * bottom + j, :, side] = unpack(CR[a, 0], CR[b, 0], 12 * j, D)
        for j in range(6):
            at = pl.ds((CH + rows) * bottom + 8 * (j % 2), 8)
            ELP[j // 2, at, side] = unpack(CR[a, 1], CR[b, 1], 16 * j, 16)
    centre(CH - 8, 16)
    centre(CH + rows - 8, 16)
    expand(D - S, S, everywhere, (0, 1))
    expand(D - S, S + 1, everywhere, (2,))
    expand(D + rows, S, everywhere, (0, 1, 2))
    for m in range(S):
        rim(m, D - S + 1)
    gram = gram + products(
        V, VB, [D + j for j in range(S)] + [D + rows - S + j for j in range(S)], own
    )

    def allsum(phase, tile, me, n, device, meanwhile):
        RB[phase, me] = tile
        for d in range(1, n):
            pltpu.make_async_remote_copy(
                src_ref=RB.at[phase, me], dst_ref=RB.at[phase, me],
                send_sem=rs.at[phase], recv_sem=rr.at[phase],
                device_id=device((me + d) % n), device_id_type=MESH,
            ).start()
        meanwhile()
        pending(phase, n).wait_recv()
        parts = [RB[phase, d] for d in range(n)]
        while len(parts) > 1:
            odd = parts[len(parts) // 2 * 2 :]
            parts = [parts[j] + parts[j + 1] for j in range(0, len(parts) - 1, 2)] + odd
        return parts[0]

    def pending(phase, n):
        some = RB.at[phase, pl.ds(0, n - 1)]
        return pltpu.make_async_remote_copy(
            src_ref=some, dst_ref=some, send_sem=rs.at[phase], recv_sem=rr.at[phase],
            device_id=(up, me_c), device_id_type=MESH,
        )

    def cast(first, count):
        for i in range(first, first + count):
            VB[i] = halves(jnp.concatenate([V[m, i] for m in range(S)], 0))

    def outer_rows():
        for n in range(10, 14):
            copies[n].wait_recv()
        centre(0, 16)
        centre(CH + rows, 16)
        expand(0, S + 1, everywhere, (0, 1, 2))
        expand(ext - S - 1, S + 1, everywhere, (0, 1, 2))
        for m in range(S - 1):
            rim(m, 1)

    def outer_cast(depth):
        cast(D - depth, depth)
        cast(D + rows, depth)

    for sweep in range(OUTER):

        def level(m, c):
            stencil_rows(V.at[m], E, L, C, D - S + 1, rows + 2 * S - 2, store(V.at[m + 1]))
            return c

        if sweep:
            lax.fori_loop(0, S, level, 0)
            gram = product_blocks(V, VB, D, rows // 8, 8, own)
        depth = S * (OUTER - 1 - sweep)
        tile = moments(gram)
        tile = allsum(
            2 * sweep, tile, me_c, nc, lambda c: (me_r, c),
            outer_rows if sweep == 0 else lambda: outer_cast(depth + 1),
        )
        tile = allsum(
            2 * sweep + 1, tile, me_r, nr, lambda r: (r, me_c),
            (lambda: outer_cast(depth + 1)) if sweep == 0 else lambda: None,
        )
        if sweep == 0:
            for copy in copies:
                copy.wait_send()
        X = (X1, X2)[sweep]
        count = rows + 2 * depth + 2
        combine(VB, solve(tile), X, D - depth - 1, count, 11 if count % 11 == 0 else 17)

        def update(i, x):
            V[0, i] = V[0, i] - SHIFT * (x + X[i])

        stencil_rows(X, E, L, C, D - depth, rows + 2 * depth, update)

    for r0, c0 in tiles:
        rsl, sl = pl.ds(r0, 8), pl.ds(c0, LANES)
        at = pl.ds(D + r0, 8)
        xo[:, rsl, sl] = jnp.swapaxes(X1[at, :, sl] + X2[at, :, sl], 0, 1)
        ro[:, rsl, sl] = jnp.swapaxes(V[0, at, :, sl], 0, 1)
    for phase in range(2 * OUTER):
        pending(phase, (nc, nr)[phase % 2]).wait_send()


def local(right_side, east_class, lower_class, via_mask, class_conductance):
    nr, nc = lax.axis_size("rows"), lax.axis_size("cols")
    loads, rows, own = right_side.shape
    ext, width, crows = rows + 2 * D, own + LANES, rows + 2 * CH
    vmem = pl.BlockSpec(memory_space=pltpu.VMEM)
    packed = rows // 8 + -(-3 * (rows // 8) // 8)
    field = pltpu.VMEM((ext, loads, width), f32)
    dma = pltpu.SemaphoreType.DMA
    return pl.pallas_call(
        functools.partial(kernel, nr, nc),
        out_shape=[jax.ShapeDtypeStruct(right_side.shape, f32)] * 2,
        in_specs=[pl.BlockSpec(memory_space=pltpu.HBM)] * 5,
        out_specs=[vmem] * 2,
        scratch_shapes=[
            pltpu.VMEM(right_side.shape, f32),
            pltpu.VMEM((rows, own), jnp.int32),
            pltpu.VMEM((rows, own), jnp.int32),
            pltpu.VMEM((rows, own), jnp.int32),
            pltpu.SMEM(class_conductance.shape, f32),
            pltpu.VMEM((S + 1, ext, loads, width), f32),
            pltpu.VMEM((ext, 2 * loads * S, width), bf16),
            field, field, field, field, field,
            pltpu.VMEM((3, crows, width), f32),
            pltpu.VMEM((crows, width), f32),
            pltpu.VMEM((2, packed, 8, LANES), f32),
            pltpu.VMEM((2, packed, 8, LANES), f32),
            pltpu.VMEM((4, 2, 8, LANES), f32),
            pltpu.VMEM((4, 2, 8, LANES), f32),
            pltpu.VMEM((2 * OUTER, max(nr, nc), 8, LANES), f32),
            dma((5,)),
            dma((14,)),
            dma((14,)),
            dma((2 * OUTER,)),
            dma((2 * OUTER,)),
        ],
        compiler_params=pltpu.CompilerParams(
            collective_id=0, has_side_effects=True, vmem_limit_bytes=40 * 2**20
        ),
    )(
        *(
            pltpu.with_memory_space_constraint(x, pltpu.HBM)
            for x in (right_side, east_class, lower_class, via_mask, class_conductance)
        )
    )


def solution(mesh):
    return jax.shard_map(
        local,
        mesh=mesh,
        in_specs=(
            P(None, "rows", "cols"),
            P("rows", "cols"),
            P("rows", "cols"),
            P("rows", "cols"),
            P(),
        ),
        out_specs=(P(None, "rows", "cols"), P(None, "rows", "cols")),
        check_vma=False,
    )
```

```python
import functools

import jax
import jax.numpy as jnp
from jax import lax
from jax.experimental import pallas as pl
from jax.experimental.pallas import tpu as pltpu
from jax.sharding import PartitionSpec as P

S = 5
OUTER = 2
D = S * OUTER
LEAK = 0.05
PAD_G = 2.0
SHIFT = 6.0
LANES = 128
CH = 16
f32 = jnp.float32
bf16 = jnp.bfloat16
MESH = pl.DeviceIdType.MESH


def lane_bc(x, lane):
    return jnp.broadcast_to(x[:, lane : lane + 1], x.shape)


def row_bc(x, row):
    return jnp.broadcast_to(x[row : row + 1, :], x.shape)


def stencil_rows(src, E, L, C, first, count, put):
    width = src.shape[-1]
    below = L[first - 1] * src[first - 1]
    for q in range(count):
        i = first + q
        v = src[i]
        e = E[i]
        l = L[i]
        out = (C[i] * v - e * pltpu.roll(v, width - 1, 1)) - (
            pltpu.roll(e * v, 1, 1) + (l * src[i + 1] + below)
        )
        put(i, v, out)
        below = l * v


def pair(x):
    high = x.astype(bf16).astype(f32)
    return jnp.concatenate([high, x - high], 0).astype(bf16)


def stacked(planes, i, lanes):
    return jnp.concatenate([plane[i][:, :lanes] for plane in planes], 0)


def products(VB, WB, lines, own):
    left, right = [], []
    for i in lines:
        left.append(stacked([VB.at[m] for m in range(S)], i - D, own))
        right.append(
            jnp.concatenate([stacked([WB.at[m] for m in range(S)], i, own), VB[0, i - D]], 0)
        )
    return lax.dot_general(
        jnp.concatenate(left, 1), jnp.concatenate(right, 1),
        (((1,), (1,)), ((), ())), preferred_element_type=f32,
    )


def product_blocks(VB, WB, first, blocks, step, own):
    def some(j, acc):
        return acc + products(VB, WB, [first + j * step + q for q in range(step)], own)

    return lax.fori_loop(0, blocks, some, jnp.zeros((16 * S, 16 * (S + 1)), f32))


def moments(acc):
    block = lax.broadcasted_iota(jnp.int32, (8, LANES), 1) >> 3
    filler = jnp.zeros((8, LANES - 16 * (S + 1)), f32)
    out = jnp.zeros((8, LANES), f32)
    for m in range(S):
        g = acc[16 * m : 16 * m + 8] + acc[16 * m + 8 : 16 * m + 16]
        g = jnp.concatenate([g, filler], 1)
        g = g + pltpu.roll(g, LANES - 8, 1)
        out = jnp.where(block == 2 * m, g, out)
        if m < S - 1:
            out = jnp.where(block == 2 * m + 1, pltpu.roll(g, LANES - 8, 1), out)
        x = g if m == 1 else pltpu.roll(g, (8 * m - 8) % LANES, 1)
        out = jnp.where(block == 9 + m, x, out)
    return out


def solve(packed):
    lane = lax.broadcasted_iota(jnp.int32, (8, LANES), 1)
    sub = lax.broadcasted_iota(jnp.int32, (8, LANES), 0)
    T = [packed if m == 0 else pltpu.roll(packed, LANES - 8 * m, 1) for m in range(S)]
    T.append(pltpu.roll(packed, LANES - 72, 1) * (1.0 / SHIFT))
    for kb in range(S):
        base = 8 * kb
        cols = {m: [lane_bc(T[m], base + j) for j in range(8)] for m in range(kb, S + 1)}
        piv = list(cols[kb])
        within = (lane >= base) & (lane < base + 8)
        g = jnp.where(within, jnp.where(lane - base == sub, -1.0, 0.0), T[kb])
        for k in range(8):
            inv = 1.0 / row_bc(piv[k], k)
            here = sub == k
            for j in range(k + 1, 8):
                r = row_bc(piv[j], k) * inv
                piv[j] = jnp.where(here, r, piv[j] - piv[k] * r)
            r = row_bc(g, k) * inv
            g = jnp.where(here, r, g - piv[k] * r)
        q = [row_bc(g, a) for a in range(8)]
        for m in range(kb + 1, S + 1):
            s0 = cols[m][0] * q[0]
            s1 = cols[m][1] * q[1]
            for a in range(2, 8, 2):
                s0 = s0 + cols[m][a] * q[a]
                s1 = s1 + cols[m][a + 1] * q[a + 1]
            T[m] = jnp.where(within, 0.0, T[m]) - (s0 + s1)
    return T[S]


def weights(coefficients):
    block = lax.broadcasted_iota(jnp.int32, (8, LANES), 1) >> 3
    moved = [coefficients] + [pltpu.roll(coefficients, 8 * j, 1) for j in range(1, S + 1)]
    x = jnp.zeros((8, LANES), f32)
    for m in range(S):
        x = jnp.where(block == 2 * m, moved[m], x)
        x = jnp.where(block == 2 * m + 1, moved[m + 1], x)
    return pair(x)[:, : 16 * S]


def combine(left, right, first, rows, step, put):
    def some(j, c):
        for q in range(step):
            i = first + j * step + q
            out = lax.dot_general(
                left, right(i), (((1,), (0,)), ((), ())), preferred_element_type=f32
            )
            put(i, out[:8] + out[8:])
        return c

    lax.fori_loop(0, rows // step, some, 0)


def kernel(
    nr, nc, rhs_in, ecls_in, lcls_in, via_in, table_in, xo, ro,
    rhs, ecls, lcls, via, table,
    V, VBS, WB, E, L, C, X, ELP, CP, PS, PR, CS, CR, RB, ls, hs, hr, rs, rr,
):
    rows, own = rhs.shape[1], rhs.shape[2]
    ext = rows + 2 * D
    width = own + LANES
    me_r = lax.axis_index("rows")
    me_c = lax.axis_index("cols")
    up, down = (me_r + nr - 1) % nr, (me_r + 1) % nr
    west, east = (me_c + nc - 1) % nc, (me_c + 1) % nc

    loads = []
    for j, (src, dst) in enumerate(
        ((rhs_in, rhs), (ecls_in, ecls), (lcls_in, lcls), (via_in, via), (table_in, table))
    ):
        loads.append(pltpu.make_async_copy(src, dst, ls.at[j]))
        loads[-1].start()

    barrier = pltpu.get_barrier_semaphore()

    def greet(r, c):
        pl.semaphore_signal(barrier, inc=1, device_id=(r, c), device_id_type=MESH)

    for r in (up, down):
        for c in (west, east):
            greet(r, c)
    for d in range(1, nc):
        greet(me_r, (me_c + d) % nc)
    for d in range(1, nr):
        greet((me_r + d) % nr, me_c)

    copies = [None] * 14

    def send(n, src, dst, r, c):
        copies[n] = pltpu.make_async_remote_copy(
            src_ref=src, dst_ref=dst, send_sem=hs.at[n], recv_sem=hr.at[n],
            device_id=(r, c), device_id_type=MESH,
        )
        copies[n].start()

    lane = lax.broadcasted_iota(jnp.int32, (8, LANES), 1)
    tiles = [(8 * g, LANES * t) for g in range(rows // 8) for t in range(own // LANES)]
    body = pl.ds(0, own)
    ends = (pl.ds(0, LANES), pl.ds(own - LANES, LANES))

    def transpose_in(chosen):
        for r0, c0 in chosen:
            V[0, pl.ds(D + r0, 8), :, pl.ds(c0, LANES)] = jnp.swapaxes(
                rhs[:, pl.ds(r0, 8), pl.ds(c0, LANES)], 0, 1
            )

    def look_up(chosen):
        for r0, c0 in chosen:
            rsl, sl = pl.ds(r0, 8), pl.ds(c0, LANES)
            row_id = lax.broadcasted_iota(jnp.int32, (8, LANES), 0) + (me_r * rows + r0)
            col_id = lane + (me_c * own + c0)
            ec, lc = ecls[rsl, sl], lcls[rsl, sl]
            e = jnp.zeros((8, LANES), f32)
            l = jnp.zeros((8, LANES), f32)
            for k in range(table.shape[0]):
                e = jnp.where(ec == k, table[k], e)
                l = jnp.where(lc == k, table[k], l)
            at = pl.ds(CH + r0, 8)
            ELP[0, at, sl] = jnp.where(col_id < nc * own - 1, e, 0.0)
            ELP[1, at, sl] = jnp.where(row_id < nr * rows - 1, l, 0.0)
            ELP[2, at, sl] = PAD_G * via[rsl, sl].astype(f32)

    border = [at for at in tiles if at[0] in (0, rows - 8)]
    others = [at for at in tiles if at not in border]
    loads[0].wait()
    transpose_in(border)
    pl.semaphore_wait(barrier, nr + nc + 2)
    send(0, V.at[0, pl.ds(D, S), :, body], V.at[0, pl.ds(D + rows, S), :, body], up, me_c)
    send(1, V.at[0, pl.ds(D + rows - S, S), :, body], V.at[0, pl.ds(D - S, S), :, body], down, me_c)
    for load in loads[1:]:
        load.wait()
    look_up(border)
    send(4, ELP.at[:, pl.ds(CH, 8), body], ELP.at[:, pl.ds(CH + rows, 8), body], up, me_c)
    send(5, ELP.at[:, pl.ds(CH + rows - 8, 8), body], ELP.at[:, pl.ds(CH - 8, 8), body], down, me_c)
    transpose_in(others)
    look_up(others)

    def pack(pieces, gap, skip):
        x = jnp.zeros((8, LANES), f32)
        for j, piece in enumerate(pieces):
            x = jnp.where(lane >= gap * j, pltpu.roll(piece, (gap * j + skip) % LANES, 1), x)
        return x

    ntile = rows // 8
    for right, sl in enumerate(ends):
        for g in range(ntile):
            PS[right, g] = pack([V[0, D + 8 * g + j, :, sl] for j in range(8)], 16, D * right)
        planes = [ELP[p, pl.ds(CH + 8 * g, 8), sl] for p in range(3) for g in range(ntile)]
        for q in range(0, len(planes), 8):
            PS[right, ntile + q // 8] = pack(planes[q : q + 8], 16, 16 * right)
        for bottom in range(2):
            n = 2 * bottom + right
            i, c = (rows, rows) if bottom else (D, CH)
            CS[n, 0] = pack([V[0, i + j, :, sl] for j in range(D)], 12, D * right)
            CS[n, 1] = pack(
                [ELP[j // 2, pl.ds(c + 8 * (j % 2), 8), sl] for j in range(6)], 16, 16 * right
            )

    send(2, PS.at[0], PR.at[0], me_r, west)
    send(3, PS.at[1], PR.at[1], me_r, east)
    for n in range(4):
        send(6 + n, CS.at[n], CR.at[n], down if n // 2 else up, east if n % 2 else west)
    send(10, V.at[0, pl.ds(D + S, S), :, body], V.at[0, pl.ds(D + rows + S, S), :, body], up, me_c)
    send(11, V.at[0, pl.ds(rows, S), :, body], V.at[0, pl.ds(0, S), :, body], down, me_c)
    send(12, ELP.at[:, pl.ds(CH + 8, 8), body], ELP.at[:, pl.ds(CH + rows + 8, 8), body], up, me_c)
    send(13, ELP.at[:, pl.ds(rows, 8), body], ELP.at[:, pl.ds(0, 8), body], down, me_c)

    scale = 1.0 / SHIFT
    side = pl.ds(own, LANES)
    everywhere = pl.ds(0, width)
    left = lane < LANES // 2

    def expand(first, count, sl, planes):
        for i in range(first, first + count):
            for p in planes:
                at = pl.ds(i + CH - D, 1)
                x = ELP[p, at, sl] * scale if p < 2 else CP[at, sl]
                (E, L, C)[p][i, :, sl] = jnp.broadcast_to(x, (8, sl.size))

    def centre(first, count):
        at = pl.ds(first, count)
        e, l = ELP[0, at], ELP[1, at]
        around = (e + pltpu.roll(e, 1, 1)) + (l + pltpu.roll(l, 1, 0))
        CP[at] = (around + (ELP[2, at] + LEAK)) * scale - 1.0

    def unpack(east_piece, west_piece, shift, wide):
        return jnp.where(
            left,
            pltpu.roll(east_piece, (LANES - shift) % LANES, 1),
            pltpu.roll(west_piece, (LANES - wide - shift) % LANES, 1),
        )

    def level(m, VB, first, count, widest):
        def put(i, v, out):
            V[m + 1, i] = out
            if D <= i < D + rows:
                VB[m, i - D] = pair(v[:, :own])
            if widest <= i < ext - widest:
                WB[m, i] = pair(v + out)

        stencil_rows(V.at[m], E, L, C, first, count, put)

    def rim(m, VB, outside):
        for first in (outside + m, ext - outside - m - S):
            level(m, VB, first, S, D - S)

    expand(D, rows, body, (0, 1))
    for n in (2, 3):
        copies[n].wait_recv()
    for i in range(rows):
        V[0, D + i, :, side] = unpack(PR[0, i // 8], PR[1, i // 8], 16 * (i % 8), D)
    for j in range(3 * ntile):
        q = ntile + j // 8
        ELP[j // ntile, pl.ds(CH + 8 * (j % ntile), 8), side] = unpack(
            PR[0, q], PR[1, q], 16 * (j % 8), 16
        )
    centre(CH, rows)
    expand(D, rows, side, (0, 1))
    expand(D + 1, rows - 1, everywhere, (2,))

    VB = VBS.at[0]

    def inner_level(m, c):
        level(m, VB, D + 1, rows - 2, D - S)
        return c

    lax.fori_loop(0, S, inner_level, 0)
    gram = product_blocks(VB, WB, D + S, 2, (rows - 2 * S) // 2, own)

    for n in (0, 1, 4, 5, 6, 7, 8, 9):
        copies[n].wait_recv()
    for bottom in range(2):
        a, b = 2 - 2 * bottom, 3 - 2 * bottom
        for j in range(D):
            V[0, (D + rows) * bottom + j, :, side] = unpack(CR[a, 0], CR[b, 0], 12 * j, D)
        for j in range(6):
            at = pl.ds((CH + rows) * bottom + 8 * (j % 2), 8)
            ELP[j // 2, at, side] = unpack(CR[a, 1], CR[b, 1], 16 * j, 16)
    centre(CH - 8, 16)
    centre(CH + rows - 8, 16)
    expand(D - S, S, everywhere, (0, 1))
    expand(D - S, S + 1, everywhere, (2,))
    expand(D + rows, S, everywhere, (0, 1, 2))
    for m in range(S):
        rim(m, VB, D - S + 1)
    gram = gram + products(
        VB, WB, [D + j for j in range(S)] + [D + rows - S + j for j in range(S)], own
    )

    def allsum(phase, tile, me, n, device, meanwhile):
        RB[phase, me] = tile
        for d in range(1, n):
            pltpu.make_async_remote_copy(
                src_ref=RB.at[phase, me], dst_ref=RB.at[phase, me],
                send_sem=rs.at[phase], recv_sem=rr.at[phase],
                device_id=device((me + d) % n), device_id_type=MESH,
            ).start()
        meanwhile()
        pending(phase, n).wait_recv()
        parts = [RB[phase, d] for d in range(n)]
        while len(parts) > 1:
            odd = parts[len(parts) // 2 * 2 :]
            parts = [parts[j] + parts[j + 1] for j in range(0, len(parts) - 1, 2)] + odd
        return parts[0]

    def pending(phase, n):
        some = RB.at[phase, pl.ds(0, n - 1)]
        return pltpu.make_async_remote_copy(
            src_ref=some, dst_ref=some, send_sem=rs.at[phase], recv_sem=rr.at[phase],
            device_id=(up, me_c), device_id_type=MESH,
        )

    def outer_rows():
        for n in range(10, 14):
            copies[n].wait_recv()
        centre(0, 16)
        centre(CH + rows, 16)
        expand(0, S + 1, everywhere, (0, 1, 2))
        expand(ext - S - 1, S + 1, everywhere, (0, 1, 2))
        for m in range(S):
            rim(m, VBS.at[0], 1)

    def images(i):
        return stacked([WB.at[m] for m in range(S)], i, width)

    def bases(sweep, i):
        return stacked([VBS.at[sweep, m] for m in range(S)], i - D, own)

    def set_residual(i, x):
        V[0, i] = V[0, i] - SHIFT * x

    def set_solution(i, x):
        X[i - D] = x

    def reduce(tile, sweep, meanwhile):
        tile = allsum(2 * sweep, tile, me_c, nc, lambda c: (me_r, c), meanwhile)
        return allsum(2 * sweep + 1, tile, me_r, nr, lambda r: (r, me_c), lambda: None)

    first_left = weights(solve(reduce(moments(gram), 0, outer_rows)))
    for copy in copies:
        copy.wait_send()
    combine(first_left, images, D - S, rows + 2 * S, rows + 2 * S, set_residual)

    VB = VBS.at[1]
    half = S // 2
    for start, stop in ((0, half), (half, S)):
        lost = S - 1 - start

        def some_level(m, c):
            level(m, VB, D - lost, rows + 2 * lost, D)
            return c

        lax.fori_loop(start, stop, some_level, 0)
    gram = product_blocks(VB, WB, D, 2, rows // 2, own)
    last_left = weights(
        solve(
            reduce(
                moments(gram), 1,
                lambda: combine(first_left, lambda i: bases(0, i), D, rows, 16, set_solution),
            )
        )
    )

    def finish(i, x):
        X[i - D] = X[i - D] + x[:, :own]
        V[0, i, :, body] = V[0, i, :, body] - SHIFT * x[:, own:]

    combine(
        last_left, lambda i: jnp.concatenate([bases(1, i), images(i)[:, :own]], 1),
        D, rows, rows, finish,
    )
    for r0, c0 in tiles:
        rsl, sl = pl.ds(r0, 8), pl.ds(c0, LANES)
        xo[:, rsl, sl] = jnp.swapaxes(X[rsl, :, sl], 0, 1)
        ro[:, rsl, sl] = jnp.swapaxes(V[0, pl.ds(D + r0, 8), :, sl], 0, 1)
    for phase in range(2 * OUTER):
        pending(phase, (nc, nr)[phase % 2]).wait_send()


def local(right_side, east_class, lower_class, via_mask, class_conductance):
    nr, nc = lax.axis_size("rows"), lax.axis_size("cols")
    loads, rows, own = right_side.shape
    ext, width, crows = rows + 2 * D, own + LANES, rows + 2 * CH
    vmem = pl.BlockSpec(memory_space=pltpu.VMEM)
    packed = rows // 8 + -(-3 * (rows // 8) // 8)
    field = pltpu.VMEM((ext, loads, width), f32)
    dma = pltpu.SemaphoreType.DMA
    return pl.pallas_call(
        functools.partial(kernel, nr, nc),
        out_shape=[jax.ShapeDtypeStruct(right_side.shape, f32)] * 2,
        in_specs=[pl.BlockSpec(memory_space=pltpu.HBM)] * 5,
        out_specs=[vmem] * 2,
        scratch_shapes=[
            pltpu.VMEM(right_side.shape, f32),
            pltpu.VMEM((rows, own), jnp.int32),
            pltpu.VMEM((rows, own), jnp.int32),
            pltpu.VMEM((rows, own), jnp.int32),
            pltpu.SMEM(class_conductance.shape, f32),
            pltpu.VMEM((S + 1, ext, loads, width), f32),
            pltpu.VMEM((OUTER, S, rows, 2 * loads, own), bf16),
            pltpu.VMEM((S, ext, 2 * loads, width), bf16),
            field, field, field,
            pltpu.VMEM((rows, loads, own), f32),
            pltpu.VMEM((3, crows, width), f32),
            pltpu.VMEM((crows, width), f32),
            pltpu.VMEM((2, packed, 8, LANES), f32),
            pltpu.VMEM((2, packed, 8, LANES), f32),
            pltpu.VMEM((4, 2, 8, LANES), f32),
            pltpu.VMEM((4, 2, 8, LANES), f32),
            pltpu.VMEM((2 * OUTER, max(nr, nc), 8, LANES), f32),
            dma((5,)),
            dma((14,)),
            dma((14,)),
            dma((2 * OUTER,)),
            dma((2 * OUTER,)),
        ],
        compiler_params=pltpu.CompilerParams(
            collective_id=0, has_side_effects=True, vmem_limit_bytes=40 * 2**20
        ),
    )(
        *(
            pltpu.with_memory_space_constraint(x, pltpu.HBM)
            for x in (right_side, east_class, lower_class, via_mask, class_conductance)
        )
    )


def solution(mesh):
    return jax.shard_map(
        local,
        mesh=mesh,
        in_specs=(
            P(None, "rows", "cols"),
            P("rows", "cols"),
            P("rows", "cols"),
            P("rows", "cols"),
            P(),
        ),
        out_specs=(P(None, "rows", "cols"), P(None, "rows", "cols")),
        check_vma=False,
    )
```

```python
import functools

import jax
import jax.numpy as jnp
from jax import lax
from jax.experimental import pallas as pl
from jax.experimental.pallas import tpu as pltpu
from jax.sharding import PartitionSpec as P

S = 5
OUTER = 2
D = S * OUTER
LEAK = 0.05
PAD_G = 2.0
SHIFT = 6.0
LANES = 128
CH = 16
f32 = jnp.float32
bf16 = jnp.bfloat16
MESH = pl.DeviceIdType.MESH


def lane_bc(x, lane):
    return jnp.broadcast_to(x[:, lane : lane + 1], x.shape)


def row_bc(x, row):
    return jnp.broadcast_to(x[row : row + 1, :], x.shape)


def whole(ref, i):
    return ref[i]


def stencil_rows(src, E, L, C, first, count, put, view=whole):
    v = view(src, first)
    width = v.shape[-1]
    below = view(L, first - 1) * view(src, first - 1)
    for q in range(count):
        i = first + q
        e, l, after = view(E, i), view(L, i), view(src, i + 1)
        out = (view(C, i) * v - e * pltpu.roll(v, width - 1, 1)) - (
            pltpu.roll(e * v, 1, 1) + (l * after + below)
        )
        put(i, v, out)
        below = l * v
        v = after


def pair(x):
    high = x.astype(bf16).astype(f32)
    return jnp.concatenate([high, x - high], 0).astype(bf16)


def stacked(planes, i, pick):
    return jnp.concatenate([pick(plane[i]) for plane in planes], 0)


def products(VB, WB, lines, pick):
    left, right = [], []
    for i in lines:
        left.append(stacked([VB.at[m] for m in range(S)], i - D, pick))
        right.append(
            jnp.concatenate(
                [stacked([WB.at[m] for m in range(S)], i, pick), pick(VB[0, i - D])], 0
            )
        )
    return lax.dot_general(
        jnp.concatenate(left, 1), jnp.concatenate(right, 1),
        (((1,), (1,)), ((), ())), preferred_element_type=f32,
    )


def product_blocks(VB, WB, first, blocks, step, pick):
    def some(j, acc):
        return acc + products(VB, WB, [first + j * step + q for q in range(step)], pick)

    return lax.fori_loop(0, blocks, some, jnp.zeros((16 * S, 16 * (S + 1)), f32))


def moments(acc):
    block = lax.broadcasted_iota(jnp.int32, (8, LANES), 1) >> 3
    filler = jnp.zeros((8, LANES - 16 * (S + 1)), f32)
    out = jnp.zeros((8, LANES), f32)
    for m in range(S):
        g = acc[16 * m : 16 * m + 8] + acc[16 * m + 8 : 16 * m + 16]
        g = jnp.concatenate([g, filler], 1)
        g = g + pltpu.roll(g, LANES - 8, 1)
        out = jnp.where(block == 2 * m, g, out)
        if m < S - 1:
            out = jnp.where(block == 2 * m + 1, pltpu.roll(g, LANES - 8, 1), out)
        x = g if m == 1 else pltpu.roll(g, (8 * m - 8) % LANES, 1)
        out = jnp.where(block == 9 + m, x, out)
    return out


def solve(packed):
    lane = lax.broadcasted_iota(jnp.int32, (8, LANES), 1)
    sub = lax.broadcasted_iota(jnp.int32, (8, LANES), 0)
    T = [packed if m == 0 else pltpu.roll(packed, LANES - 8 * m, 1) for m in range(S)]
    T.append(pltpu.roll(packed, LANES - 72, 1) * (1.0 / SHIFT))
    for kb in range(S):
        base = 8 * kb
        cols = {m: [lane_bc(T[m], base + j) for j in range(8)] for m in range(kb, S + 1)}
        piv = list(cols[kb])
        within = (lane >= base) & (lane < base + 8)
        g = jnp.where(within, jnp.where(lane - base == sub, -1.0, 0.0), T[kb])
        for k in range(8):
            inv = 1.0 / row_bc(piv[k], k)
            here = sub == k
            for j in range(k + 1, 8):
                r = row_bc(piv[j], k) * inv
                piv[j] = jnp.where(here, r, piv[j] - piv[k] * r)
            r = row_bc(g, k) * inv
            g = jnp.where(here, r, g - piv[k] * r)
        q = [row_bc(g, a) for a in range(8)]
        for m in range(kb + 1, S + 1):
            s0 = cols[m][0] * q[0]
            s1 = cols[m][1] * q[1]
            for a in range(2, 8, 2):
                s0 = s0 + cols[m][a] * q[a]
                s1 = s1 + cols[m][a + 1] * q[a + 1]
            T[m] = jnp.where(within, 0.0, T[m]) - (s0 + s1)
    return T[S]


def weights(coefficients):
    block = lax.broadcasted_iota(jnp.int32, (8, LANES), 1) >> 3
    moved = [coefficients] + [pltpu.roll(coefficients, 8 * j, 1) for j in range(1, S + 1)]
    x = jnp.zeros((8, LANES), f32)
    for m in range(S):
        x = jnp.where(block == 2 * m, moved[m], x)
        x = jnp.where(block == 2 * m + 1, moved[m + 1], x)
    return pair(x)[:, : 16 * S]


def combine(left, right, first, rows, step, put):
    def some(j, c):
        for q in range(step):
            i = first + j * step + q
            out = lax.dot_general(
                left, right(i), (((1,), (0,)), ((), ())), preferred_element_type=f32
            )
            put(i, out[:8] + out[8:])
        return c

    lax.fori_loop(0, rows // step, some, 0)


def kernel(
    nr, nc, rhs_in, ecls_in, lcls_in, via_in, table_in, xo, ro,
    rhs, ecls, lcls, via, table,
    V, VBS, WB, E, L, C, X, ELP, CP, PS, PR, CS, CR, KS, KR, KF, RB, ls, hs, hr, rs, rr,
):
    rows, own = rhs.shape[1], rhs.shape[2]
    ext = rows + 2 * D
    width = own + LANES
    me_r = lax.axis_index("rows")
    me_c = lax.axis_index("cols")
    up, down = (me_r + nr - 1) % nr, (me_r + 1) % nr
    west, east = (me_c + nc - 1) % nc, (me_c + 1) % nc

    barrier = pltpu.get_barrier_semaphore()

    def greet(r, c):
        pl.semaphore_signal(barrier, inc=1, device_id=(r, c), device_id_type=MESH)

    for r, c in ((up, me_c), (down, me_c), (me_r, west), (me_r, east)):
        greet(r, c)
    for r in (up, down):
        for c in (west, east):
            greet(r, c)
    loads = []
    for j, (src, dst) in enumerate(
        ((rhs_in, rhs), (ecls_in, ecls), (lcls_in, lcls), (via_in, via), (table_in, table))
    ):
        loads.append(pltpu.make_async_copy(src, dst, ls.at[j]))
        loads[-1].start()
    for d in range(2, nc - 1):
        greet(me_r, (me_c + d) % nc)
    for d in range(2, nr - 1):
        greet((me_r + d) % nr, me_c)

    copies = [None] * 20

    def send(n, src, dst, r, c):
        copies[n] = pltpu.make_async_remote_copy(
            src_ref=src, dst_ref=dst, send_sem=hs.at[n], recv_sem=hr.at[n],
            device_id=(r, c), device_id_type=MESH,
        )
        copies[n].start()

    lane = lax.broadcasted_iota(jnp.int32, (8, LANES), 1)
    tiles = [(8 * g, LANES * t) for g in range(rows // 8) for t in range(own // LANES)]
    body = pl.ds(0, own)
    ends = (pl.ds(0, LANES), pl.ds(own - LANES, LANES))

    def transpose_in(chosen):
        for r0, c0 in chosen:
            V[0, pl.ds(D + r0, 8), :, pl.ds(c0, LANES)] = jnp.swapaxes(
                rhs[:, pl.ds(r0, 8), pl.ds(c0, LANES)], 0, 1
            )

    def look_up(chosen):
        for r0, c0 in chosen:
            rsl, sl = pl.ds(r0, 8), pl.ds(c0, LANES)
            row_id = lax.broadcasted_iota(jnp.int32, (8, LANES), 0) + (me_r * rows + r0)
            col_id = lane + (me_c * own + c0)
            ec, lc = ecls[rsl, sl], lcls[rsl, sl]
            e = jnp.zeros((8, LANES), f32)
            l = jnp.zeros((8, LANES), f32)
            for k in range(table.shape[0]):
                e = jnp.where(ec == k, table[k], e)
                l = jnp.where(lc == k, table[k], l)
            at = pl.ds(CH + r0, 8)
            ELP[0, at, sl] = jnp.where(col_id < nc * own - 1, e, 0.0)
            ELP[1, at, sl] = jnp.where(row_id < nr * rows - 1, l, 0.0)
            ELP[2, at, sl] = PAD_G * via[rsl, sl].astype(f32)

    for load in loads[1:]:
        load.wait()
    look_up(tiles)
    loads[0].wait()
    transpose_in(tiles)

    def pack(pieces, gap, skip):
        x = jnp.zeros((8, LANES), f32)
        for j, piece in enumerate(pieces):
            x = jnp.where(lane >= gap * j, pltpu.roll(piece, (gap * j + skip) % LANES, 1), x)
        return x

    ntile = rows // 8
    for right, sl in enumerate(ends):
        for g in range(ntile):
            PS[right, g] = pack([V[0, D + 8 * g + j, :, sl] for j in range(8)], 16, D * right)
        planes = [ELP[p, pl.ds(CH + 8 * g, 8), sl] for p in range(3) for g in range(ntile)]
        for q in range(0, len(planes), 8):
            PS[right, ntile + q // 8] = pack(planes[q : q + 8], 16, 16 * right)

    pl.semaphore_wait(barrier, nr + nc + 2)
    send(0, V.at[0, pl.ds(D, S), :, body], V.at[0, pl.ds(D + rows, S), :, body], up, me_c)
    send(1, V.at[0, pl.ds(D + rows - S, S), :, body], V.at[0, pl.ds(D - S, S), :, body], down, me_c)
    first8, last8 = pl.ds(CH, 8), pl.ds(CH + rows - 8, 8)
    after8, before8 = pl.ds(CH + rows, 8), pl.ds(CH - 8, 8)
    top = lax.broadcasted_iota(jnp.int32, (8, own), 0) < 4
    KS[0] = jnp.where(top, ELP[0, first8, body], pltpu.roll(ELP[2, first8, body], 4, 0))
    KS[1] = jnp.where(top, pltpu.roll(ELP[2, last8, body], 4, 0), ELP[0, last8, body])
    send(14, KS.at[0], KR.at[0], up, me_c)
    send(15, KS.at[1], KR.at[1], down, me_c)
    send(4, ELP.at[1, first8, body], ELP.at[1, after8, body], up, me_c)
    send(5, ELP.at[1, last8, body], ELP.at[1, before8, body], down, me_c)
    send(2, PS.at[0], PR.at[0], me_r, west)
    send(3, PS.at[1], PR.at[1], me_r, east)
    for right, sl in enumerate(ends):
        for bottom in range(2):
            n = 2 * bottom + right
            i, c = (rows, rows) if bottom else (D, CH)
            CS[n, 0] = pack([V[0, i + j, :, sl] for j in range(D)], 12, D * right)
            CS[n, 1] = pack(
                [ELP[j // 2, pl.ds(c + 8 * (j % 2), 8), sl] for j in range(6)], 16, 16 * right
            )
    for n in range(4):
        send(6 + n, CS.at[n], CR.at[n], down if n // 2 else up, east if n % 2 else west)
    send(10, V.at[0, pl.ds(D + S, S), :, body], V.at[0, pl.ds(D + rows + S, S), :, body], up, me_c)
    send(11, V.at[0, pl.ds(rows, S), :, body], V.at[0, pl.ds(0, S), :, body], down, me_c)
    send(12, ELP.at[:, pl.ds(CH + 8, 8), body], ELP.at[:, pl.ds(CH + rows + 8, 8), body], up, me_c)
    send(13, ELP.at[:, pl.ds(rows, 8), body], ELP.at[:, pl.ds(0, 8), body], down, me_c)
    for j, p in enumerate((0, 2)):
        send(16 + j, ELP.at[p, first8, body], KF.at[0, j], up, me_c)
        send(18 + j, ELP.at[p, last8, body], KF.at[1, j], down, me_c)

    scale = 1.0 / SHIFT
    side = pl.ds(own, LANES)
    everywhere = pl.ds(0, width)
    left = lane < LANES // 2

    def expand(first, count, sl, planes):
        for i in range(first, first + count):
            for p in planes:
                at = pl.ds(i + CH - D, 1)
                x = ELP[p, at, sl] * scale if p < 2 else CP[at, sl]
                (E, L, C)[p][i, :, sl] = jnp.broadcast_to(x, (8, sl.size))

    def centre(first, count, sl):
        at = pl.ds(first, count)
        e, l = ELP[0, at, sl], ELP[1, at, sl]
        around = (e + pltpu.roll(e, 1, 1)) + (l + pltpu.roll(l, 1, 0))
        CP[at, sl] = (around + (ELP[2, at, sl] + LEAK)) * scale - 1.0

    def unpack(east_piece, west_piece, shift, wide):
        return jnp.where(
            left,
            pltpu.roll(east_piece, (LANES - shift) % LANES, 1),
            pltpu.roll(west_piece, (LANES - wide - shift) % LANES, 1),
        )

    def level(m, VB, first, count, widest):
        def put(i, v, out):
            V[m + 1, i] = out
            if D <= i < D + rows:
                VB[m, i - D] = pair(v[:, :own])
            if widest <= i < ext - widest:
                WB[m, i] = pair(v + out)

        stencil_rows(V.at[m], E, L, C, first, count, put)

    def rim(m, VB, outside):
        for first in (outside + m, ext - outside - m - S):
            level(m, VB, first, S, D - S)

    expand(D, rows, body, (0, 1))
    centre(CH, rows, body)
    expand(D + 1, rows - 1, pl.ds(LANES, own - LANES), (2,))
    VB = VBS.at[0]
    half = S // 2
    mid = slice(LANES, own - LANES)
    spare = slice(own - LANES, own)

    def owned(x):
        return x[:, :own]

    def middle(x):
        return x[:, mid]

    def outer(x):
        return jnp.concatenate([x[:, :LANES], x[:, spare]], 1)

    def inner_levels(one):
        for start, stop in ((0, half), (half, S)):

            def some_level(m, c):
                one(m, D + 1 + start, rows - 2 - 2 * start)
                return c

            lax.fori_loop(start, stop, some_level, 0)

    def middle_level(m, first, count):
        def put(i, v, out):
            V[m + 1, i, :, body] = out
            VB[m, i - D, :, mid] = pair(middle(v))
            WB[m, i, :, mid] = pair(middle(v) + middle(out))

        stencil_rows(V.at[m], E, L, C, first, count, put, lambda ref, i: ref[i, :, body])

    def outer_level(m, first, count):
        def view(ref, i):
            return jnp.concatenate([ref[i, :, own - LANES :], ref[i, :, :LANES]], 1)

        def put(i, v, out):
            last = jnp.where(left, V[m + 1, i, :, spare], out[:, :LANES])
            start = jnp.where(left, out[:, 2 * LANES :], V[m + 1, i, :, :LANES])
            V[m + 1, i, :, own - LANES :] = jnp.concatenate([last, out[:, LANES : 2 * LANES]], 1)
            V[m + 1, i, :, :LANES] = start
            basis = pair(v)
            VB[m, i - D, :, spare] = basis[:, :LANES]
            VB[m, i - D, :, :LANES] = basis[:, 2 * LANES :]
            image = pair(v + jnp.concatenate([last, out[:, LANES : 2 * LANES], start], 1))
            WB[m, i, :, own - LANES :] = image[:, : 2 * LANES]
            WB[m, i, :, :LANES] = image[:, 2 * LANES :]

        stencil_rows(V.at[m], E, L, C, first, count, put, view)

    expand(D + 1, rows - 1, ends[0], (2,))
    inner_levels(middle_level)
    inside = (D + S, 2, (rows - 2 * S) // 2)
    gram = product_blocks(VB, WB, *inside, middle)

    for n in (2, 3):
        copies[n].wait_recv()
    for i in range(rows):
        V[0, D + i, :, side] = unpack(PR[0, i // 8], PR[1, i // 8], 16 * (i % 8), D)
    for j in range(3 * ntile):
        q = ntile + j // 8
        ELP[j // ntile, pl.ds(CH + 8 * (j % ntile), 8), side] = unpack(
            PR[0, q], PR[1, q], 16 * (j % 8), 16
        )
    centre(CH, rows, everywhere)
    expand(D, rows, side, (0, 1))
    expand(D + 1, rows - 1, side, (2,))
    expand(D + 1, rows - 1, ends[0], (2,))

    inner_levels(outer_level)
    gram = gram + product_blocks(VB, WB, *inside, outer)

    for n in (0, 1, 4, 5, 6, 7, 8, 9, 14, 15):
        copies[n].wait_recv()
    for n, at in enumerate((after8, before8)):
        ELP[0, at, body] = KR[n]
        ELP[2, at, body] = pltpu.roll(KR[n], 4, 0)
    for bottom in range(2):
        a, b = 2 - 2 * bottom, 3 - 2 * bottom
        for j in range(D):
            V[0, (D + rows) * bottom + j, :, side] = unpack(CR[a, 0], CR[b, 0], 12 * j, D)
        for j in range(6):
            at = pl.ds((CH + rows) * bottom + 8 * (j % 2), 8)
            ELP[j // 2, at, side] = unpack(CR[a, 1], CR[b, 1], 16 * j, 16)
    centre(CH - 8, 16, everywhere)
    centre(CH + rows - 8, 16, everywhere)
    expand(D - S, S, everywhere, (0, 1))
    expand(D - S, S + 1, everywhere, (2,))
    expand(D + rows, S, everywhere, (0, 1, 2))
    for m in range(S):
        rim(m, VB, D - S + 1)
    gram = gram + products(
        VB, WB, [D + j for j in range(S)] + [D + rows - S + j for j in range(S)], owned
    )

    def allsum(phase, tile, me, n, device, meanwhile):
        RB[phase, me] = tile
        for d in range(1, n):
            pltpu.make_async_remote_copy(
                src_ref=RB.at[phase, me], dst_ref=RB.at[phase, me],
                send_sem=rs.at[phase], recv_sem=rr.at[phase],
                device_id=device((me + d) % n), device_id_type=MESH,
            ).start()
        meanwhile()
        pending(phase, n).wait_recv()
        parts = [RB[phase, d] for d in range(n)]
        while len(parts) > 1:
            odd = parts[len(parts) // 2 * 2 :]
            parts = [parts[j] + parts[j + 1] for j in range(0, len(parts) - 1, 2)] + odd
        return parts[0]

    def pending(phase, n):
        some = RB.at[phase, pl.ds(0, n - 1)]
        return pltpu.make_async_remote_copy(
            src_ref=some, dst_ref=some, send_sem=rs.at[phase], recv_sem=rr.at[phase],
            device_id=(up, me_c), device_id_type=MESH,
        )

    def outer_rows():
        for n in (10, 11, 12, 13, 16, 17, 18, 19):
            copies[n].wait_recv()
        for n, at in enumerate((after8, before8)):
            ELP[0, at, body] = KF[n, 0]
            ELP[2, at, body] = KF[n, 1]
        centre(0, 16, everywhere)
        centre(CH + rows, 16, everywhere)
        expand(0, S + 1, everywhere, (0, 1, 2))
        expand(ext - S - 1, S + 1, everywhere, (0, 1, 2))
        for m in range(S):
            rim(m, VBS.at[0], 1)

    def images(i):
        return stacked([WB.at[m] for m in range(S)], i, lambda x: x)

    def bases(sweep, i):
        return stacked([VBS.at[sweep, m] for m in range(S)], i - D, lambda x: x)

    def set_residual(i, x):
        V[0, i] = V[0, i] - SHIFT * x

    def set_solution(i, x):
        X[i - D] = x

    def reduce(tile, sweep, meanwhile):
        tile = allsum(2 * sweep, tile, me_c, nc, lambda c: (me_r, c), meanwhile)
        return allsum(2 * sweep + 1, tile, me_r, nr, lambda r: (r, me_c), lambda: None)

    first_left = weights(solve(reduce(moments(gram), 0, outer_rows)))
    for copy in copies:
        copy.wait_send()
    combine(first_left, images, D - S, rows + 2 * S, rows + 2 * S, set_residual)

    VB = VBS.at[1]
    for start, stop in ((0, half), (half, S)):
        lost = S - 1 - start

        def some_level(m, c):
            level(m, VB, D - lost, rows + 2 * lost, D)
            return c

        lax.fori_loop(start, stop, some_level, 0)
    gram = product_blocks(VB, WB, D, 2, rows // 2, owned)
    last_left = weights(
        solve(
            reduce(
                moments(gram), 1,
                lambda: combine(first_left, lambda i: bases(0, i), D, rows, 16, set_solution),
            )
        )
    )

    def finish(i, x):
        X[i - D] = X[i - D] + x[:, :own]
        V[0, i, :, body] = V[0, i, :, body] - SHIFT * x[:, own:]

    combine(
        last_left, lambda i: jnp.concatenate([bases(1, i), images(i)[:, :own]], 1),
        D, rows, rows, finish,
    )
    for r0, c0 in tiles:
        rsl, sl = pl.ds(r0, 8), pl.ds(c0, LANES)
        xo[:, rsl, sl] = jnp.swapaxes(X[rsl, :, sl], 0, 1)
        ro[:, rsl, sl] = jnp.swapaxes(V[0, pl.ds(D + r0, 8), :, sl], 0, 1)
    for phase in range(2 * OUTER):
        pending(phase, (nc, nr)[phase % 2]).wait_send()


def local(right_side, east_class, lower_class, via_mask, class_conductance):
    nr, nc = lax.axis_size("rows"), lax.axis_size("cols")
    loads, rows, own = right_side.shape
    ext, width, crows = rows + 2 * D, own + LANES, rows + 2 * CH
    vmem = pl.BlockSpec(memory_space=pltpu.VMEM)
    packed = rows // 8 + -(-3 * (rows // 8) // 8)
    field = pltpu.VMEM((ext, loads, width), f32)
    dma = pltpu.SemaphoreType.DMA
    return pl.pallas_call(
        functools.partial(kernel, nr, nc),
        out_shape=[jax.ShapeDtypeStruct(right_side.shape, f32)] * 2,
        in_specs=[pl.BlockSpec(memory_space=pltpu.HBM)] * 5,
        out_specs=[vmem] * 2,
        scratch_shapes=[
            pltpu.VMEM(right_side.shape, f32),
            pltpu.VMEM((rows, own), jnp.int32),
            pltpu.VMEM((rows, own), jnp.int32),
            pltpu.VMEM((rows, own), jnp.int32),
            pltpu.SMEM(class_conductance.shape, f32),
            pltpu.VMEM((S + 1, ext, loads, width), f32),
            pltpu.VMEM((OUTER, S, rows, 2 * loads, own), bf16),
            pltpu.VMEM((S, ext, 2 * loads, width), bf16),
            field, field, field,
            pltpu.VMEM((rows, loads, own), f32),
            pltpu.VMEM((3, crows, width), f32),
            pltpu.VMEM((crows, width), f32),
            pltpu.VMEM((2, packed, 8, LANES), f32),
            pltpu.VMEM((2, packed, 8, LANES), f32),
            pltpu.VMEM((4, 2, 8, LANES), f32),
            pltpu.VMEM((4, 2, 8, LANES), f32),
            pltpu.VMEM((2, 8, own), f32),
            pltpu.VMEM((2, 8, own), f32),
            pltpu.VMEM((2, 2, 8, own), f32),
            pltpu.VMEM((2 * OUTER, max(nr, nc), 8, LANES), f32),
            dma((5,)),
            dma((20,)),
            dma((20,)),
            dma((2 * OUTER,)),
            dma((2 * OUTER,)),
        ],
        compiler_params=pltpu.CompilerParams(
            collective_id=0, has_side_effects=True, vmem_limit_bytes=40 * 2**20
        ),
    )(
        *(
            pltpu.with_memory_space_constraint(x, pltpu.HBM)
            for x in (right_side, east_class, lower_class, via_mask, class_conductance)
        )
    )


def solution(mesh):
    return jax.shard_map(
        local,
        mesh=mesh,
        in_specs=(
            P(None, "rows", "cols"),
            P("rows", "cols"),
            P("rows", "cols"),
            P("rows", "cols"),
            P(),
        ),
        out_specs=(P(None, "rows", "cols"), P(None, "rows", "cols")),
        check_vma=False,
    )
```
